512 devices in a mesh: gy: 32 (over z, y_lo), gx: 16 (over y_hi, x, core).
Axes of the slice: x: 4, y: 8 (y_hi: 2, y_lo: 4; y = y_hi * 4 + y_lo), z: 8, core: 2. Of those that a mesh axis runs over, the one named last changes fastest.
Arguments:
- tokens: bfloat16 [256, 256, 384], P('gy', 'gx'), may hold values from -6 to 6
- norm_gain: float32 [384], replicated, may hold values from 0.25 to 1.75
- norm_bias: float32 [384], replicated, may hold values from -1.5 to 1.5
- w_in: bfloat16 [384, 1536], replicated, may hold values from -0.3125 to 0.3125
- conv_taps: float32 [9, 768], replicated, may hold values from -3.5 to 3.5
- conv_bias: float32 [768], replicated, may hold values from -1.5 to 1.5
- w_x: bfloat16 [4, 768, 40], replicated, may hold values from -0.21875 to 0.21875
- w_dt: bfloat16 [4, 24, 768], replicated, may hold values from -1.25 to 1.25
- dt_bias: float32 [4, 768], replicated, may hold values from -1 to 0.5
- a_log: float32 [4, 8, 768], replicated, may hold values from -10 to -2
- d_skip: float32 [4, 768], replicated, may hold values from 0.5 to 1.5
- out_gain: float32 [768], replicated, may hold values from 0.25 to 1.75
- out_bias: float32 [768], replicated, may hold values from -1.5 to 1.5
- w_out: bfloat16 [768, 384], replicated, may hold values from -0.21875 to 0.21875
Outputs:
- mixed: bfloat16 [256, 256, 384], P('gy', 'gx')
The draws below stay inside these ranges and needn't reach their ends.
All inputs are finite; a program needn't handle non-finite values.
Results may differ from the reference program's by a relative error of at most 0.0055.
The reference program's roundings to bfloat16 on the way (of `normed`, `projected`, `conved`, `low` and `gated`) count: a program that leaves them out, or rounds other values in their place, can miss the bound.
Values may be sent and summed in bfloat16 or wider, within the bound.
A program may use at most 192 MiB of HBM per device.

```python
import math
import jax
import jax.numpy as jnp
from jax import lax

C = 384
E = 768
STATE = 8
DTR = 24
DIRS = 4
NY = 256
NX = 256


def draw_a_log(key, part):
    key = jax.random.fold_in(key, 11)
    first, second, third = jax.random.split(key, 3)
    share = 0.5
    slow = jax.random.uniform(first, (DIRS, STATE, E), jnp.float32) < share
    lengths = jnp.array([NX, NX, NY, NY], jnp.float32)[:, None, None]
    slow_rate = jnp.exp(jax.random.uniform(second, (DIRS, STATE, E), jnp.float32, math.log(0.3), 0.0)) / lengths
    fast_rate = jnp.exp(jax.random.uniform(third, (DIRS, STATE, E), jnp.float32, math.log(1.0 / 60.0), math.log(1.0 / 20.0)))
    return jnp.log(jnp.where(slow, slow_rate, fast_rate)).astype(jnp.float32)


def shard_levels(stream_key, shape, cuts, low, top_value):
    factor_of, own = 1.0, jax.random.fold_in(stream_key, 6)
    for position, parts in cuts:
        draws = jnp.exp(jax.random.uniform(jax.random.fold_in(own, position), (parts,), jnp.float32, low / len(cuts), top_value / len(cuts)))
        factor_of = factor_of * jnp.repeat(draws, shape[position] // parts).reshape([-1 if axis == position else 1 for axis in range(len(shape))])
    return factor_of


def noise(rng, dims, scale, bound, shards=(), dtype=jnp.bfloat16):
    values = scale * jax.random.normal(rng, dims, jnp.float32)
    if shards:
        values = values * shard_levels(rng, dims, shards, -0.22, 0.18)
    return jnp.clip(values, -bound, bound).astype(dtype)


def setup_inputs(seed: int = 0) -> dict:
    splits = jax.random.split(jax.random.key(seed), 15)
    return {
        "tokens": noise(splits[0], (NY, NX, C), 1.0, 6.0, ((0, 32), (1, 16))),
        "norm_gain": jnp.clip(1.0 + 0.15 * jax.random.normal(splits[1], (C,), jnp.float32), 0.25, 1.75),
        "norm_bias": noise(splits[2], (C,), 0.3, 1.5, (), jnp.float32),
        "w_in": noise(splits[3], (C, 2 * E), C ** -0.5, 0.3125),
        "conv_taps": noise(splits[4], (9, E), 3 ** -0.5, 3.5, (), jnp.float32),
        "conv_bias": noise(splits[5], (E,), 0.3, 1.5, (), jnp.float32),
        "w_x": noise(splits[6], (DIRS, E, DTR + 2 * STATE), E ** -0.5, 0.21875),
        "w_dt": noise(splits[7], (DIRS, DTR, E), DTR ** -0.5, 1.25),
        "dt_bias": jnp.clip(jax.random.uniform(splits[8], (DIRS, E), jnp.float32, -1.0, 0.5), -1.0, 0.5),
        "a_log": draw_a_log(jax.random.fold_in(splits[14], 71), 0),
        "d_skip": jnp.clip(jax.random.uniform(splits[10], (DIRS, E), jnp.float32, 0.5, 1.5), 0.5, 1.5),
        "out_gain": jnp.clip(1.0 + 0.15 * jax.random.normal(splits[11], (E,), jnp.float32), 0.25, 1.75),
        "out_bias": noise(splits[12], (E,), 0.3, 1.5, (), jnp.float32),
        "w_out": noise(splits[13], (E, C), E ** -0.5, 0.21875),
    }


def layer_norm(values, gain, bias):
    mean = lax.optimization_barrier(jnp.mean(values, axis=-1, keepdims=True))
    centred = values - mean
    spread = lax.optimization_barrier(jnp.mean(centred * centred, axis=-1, keepdims=True))
    return centred * lax.rsqrt(spread + 1e-05) * gain + bias

def line_scan(inputs, steps, in_maps, out_maps, rates):

    def advance(state, items):
        value, step, in_map, out_map = items
        decay = jnp.exp(step[None] * rates[:, None, :])
        state = decay * state + in_map.T[:, :, None] * (step * value)[None]
        return (state, lax.optimization_barrier(jnp.sum(out_map.T[:, :, None] * state, axis=0)))
    start = jnp.zeros((rates.shape[0], inputs.shape[1], inputs.shape[2]), jnp.float32)
    _, outputs = lax.scan(advance, start, (inputs, steps, in_maps, out_maps))
    return outputs

def orient(array, direction):
    if direction < 2:
        array = jnp.transpose(array, (1, 0, 2))
    if direction % 2 == 1:
        array = array[::-1]
    return array

def unorient(array, direction):
    if direction % 2 == 1:
        array = array[::-1]
    if direction < 2:
        array = jnp.transpose(array, (1, 0, 2))
    return array

def reference(tokens, norm_gain, norm_bias, w_in, conv_taps, conv_bias, w_x, w_dt, dt_bias, a_log, d_skip, out_gain, out_bias, w_out):
    height, width, chans = tokens.shape
    inner_width = w_in.shape[1] // 2
    rank = w_dt.shape[1]
    states = a_log.shape[1]
    token_float = tokens.astype(jnp.float32)
    normed = layer_norm(token_float, norm_gain, norm_bias).astype(jnp.bfloat16)
    projected = jnp.dot(normed.reshape(-1, chans), w_in, preferred_element_type=jnp.float32).astype(jnp.bfloat16)
    projected = projected.reshape(height, width, 2 * inner_width)
    inner = projected[..., :inner_width]
    gate = projected[..., inner_width:]
    padded = jnp.pad(inner, ((1, 1), (1, 1), (0, 0)))
    conv_sum = jnp.zeros((height, width, inner_width), jnp.float32) + conv_bias
    for row_tap in range(3):
        for col_tap in range(3):
            conv_sum = conv_sum + padded[row_tap:row_tap + height, col_tap:col_tap + width] * conv_taps[3 * row_tap + col_tap]
    conved = jax.nn.silu(conv_sum).astype(jnp.bfloat16)
    conved_flat = conved.reshape(-1, inner_width)
    conved_float = conved.astype(jnp.float32)
    summed = jnp.zeros((height, width, inner_width), jnp.float32)
    for direction in range(4):
        proj = jnp.dot(conved_flat, w_x[direction], preferred_element_type=jnp.float32)
        low = proj[:, :rank].astype(jnp.bfloat16)
        in_maps = proj[:, rank:rank + states].reshape(height, width, states)
        out_maps = proj[:, rank + states:].reshape(height, width, states)
        steps = jax.nn.softplus(jnp.dot(low, w_dt[direction], preferred_element_type=jnp.float32) + dt_bias[direction])
        steps = steps.reshape(height, width, inner_width)
        rates = -jnp.exp(a_log[direction])
        outputs = line_scan(orient(conved_float, direction), orient(steps, direction), orient(in_maps, direction), orient(out_maps, direction), rates)
        summed = summed + unorient(outputs, direction) + d_skip[direction] * conved_float
    gated = (layer_norm(summed, out_gain, out_bias) * jax.nn.silu(gate.astype(jnp.float32))).astype(jnp.bfloat16)
    result = token_float + jnp.dot(gated.reshape(-1, inner_width), w_out, preferred_element_type=jnp.float32).reshape(height, width, chans)
    return result.astype(jnp.bfloat16)
```

```python
import functools

import jax
import jax.numpy as jnp
from jax import lax
from jax.experimental import pallas as pl
from jax.experimental.pallas import tpu as pltpu
from jax.sharding import PartitionSpec as P

MESH = pl.DeviceIdType.MESH
F32 = jnp.float32
BF16 = jnp.bfloat16
LOG2E = 1.4426950408889634
ROWS, COLS = 8, 16
LINE = 128
LANES = 128


def rounded(value):
    return value.astype(BF16).astype(F32)


def unit_norm(values):
    mean = jnp.mean(values, axis=-1, keepdims=True)
    centred = values - mean
    spread = jnp.mean(centred * centred, axis=-1, keepdims=True)
    return centred * lax.rsqrt(spread + 1e-05)


def softplus(value):
    return jnp.maximum(value, 0.0) + jnp.log1p(jnp.exp(-jnp.abs(value)))


def silu(value):
    return value / (1.0 + jnp.exp(-value))


def kernel(
    tokens, norm_gain, norm_bias, w_in, taps, conv_bias, w_xt, w_dt, dt_bias, a_log, d_skip, out_gain, out_bias, w_out,
    out,
    edge, edge_row, edge_col, halo, padded, conved, summed, gate, row_out, col_out, row_in, col_in,
    steps, drive, in_map, out_map, row_sum, col_sum, state_out, state_in,
    row_back_out, col_back_out, row_back_in, col_back_in,
    edge_send, edge_recv, row_send, row_recv, col_send, col_recv, state_send, state_recv,
    row_back_send, row_back_recv, col_back_send, col_back_recv,
):
    ny, nx = lax.axis_size("gy"), lax.axis_size("gx")
    my_y, my_x = lax.axis_index("gy"), lax.axis_index("gx")
    half_x, member_x = my_x // ROWS, lax.rem(my_x, ROWS)
    half_y, member_y = my_y // COLS, lax.rem(my_y, COLS)
    north, south = lax.rem(my_y + ny - 1, ny), lax.rem(my_y + 1, ny)
    west, east = lax.rem(my_x + nx - 1, nx), lax.rem(my_x + 1, nx)
    over_x = (my_y, lax.rem(my_x + ROWS, nx))
    over_y = (lax.rem(my_y + COLS, ny), my_x)
    around = [(north, my_x), (south, my_x), (my_y, west), (my_y, east), (north, west), (north, east), (south, west), (south, east)]

    def in_row(member):
        return (my_y, half_x * ROWS + member)

    def in_col(member):
        return (half_y * COLS + member, my_x)

    barrier = pltpu.get_barrier_semaphore()

    def greet(device):
        pl.semaphore_signal(barrier, inc=1, device_id=device, device_id_type=MESH)

    for device in around + [over_x, over_y]:
        greet(device)

    def greet_row(turn, carry):
        greet(in_row(lax.rem(member_x + turn, ROWS)))
        return carry

    def greet_col(turn, carry):
        greet(in_col(lax.rem(member_y + turn, COLS)))
        return carry

    lax.fori_loop(1, ROWS, greet_row, 0)
    lax.fori_loop(1, COLS, greet_col, 0)

    def copy(src, dst, send, recv, device):
        return pltpu.make_async_remote_copy(
            src_ref=src, dst_ref=dst, send_sem=send, recv_sem=recv, device_id=device, device_id_type=MESH
        )

    token_float = tokens[...].astype(F32)
    for r in range(ROWS):
        edge_col[0, r : r + 1, :] = token_float[r, 0:1, :]
        edge_col[1, r : r + 1, :] = token_float[r, COLS - 1 : COLS, :]
    edge_row[0] = tokens[0]
    edge_row[1] = tokens[ROWS - 1]
    pl.semaphore_wait(barrier, 10 + ROWS - 1 + COLS - 1)
    sends = [
        (edge_row.at[0], halo.at[1], 1, around[0]),
        (edge_row.at[1], halo.at[0], 0, around[1]),
        (edge_col.at[0], edge.at[1], 3, around[2]),
        (edge_col.at[1], edge.at[0], 2, around[3]),
        (edge_col.at[0], edge.at[5], 7, around[4]),
        (edge_col.at[1], edge.at[4], 6, around[5]),
        (edge_col.at[0], edge.at[3], 5, around[6]),
        (edge_col.at[1], edge.at[2], 4, around[7]),
    ]
    edges = [copy(src, dst, edge_send.at[slot], edge_recv.at[slot], device) for src, dst, slot, device in sends]
    for item in edges:
        item.start()

    gain, bias = norm_gain[...], norm_bias[...]

    def project(cells, weight):
        normed = (unit_norm(cells) * gain + bias).astype(BF16)
        return rounded(jnp.dot(normed, weight, preferred_element_type=F32))

    cells = token_float.reshape(ROWS * COLS, -1)
    normed = (unit_norm(cells) * gain + bias).astype(BF16)
    width = gate.shape[1]
    hw, groups = width // 2, width // LANES
    inner = rounded(jnp.dot(normed, w_in[:, :width], preferred_element_type=F32))
    padded[1 : 1 + ROWS, 8 : 8 + COLS, :] = inner.reshape(ROWS, COLS, width)
    gate[...] = rounded(jnp.dot(normed, w_in[:, width:], preferred_element_type=F32))

    for item in edges:
        item.wait_recv()
    rim = jnp.concatenate(
        [
            halo[0].astype(F32), halo[1].astype(F32), edge[0], edge[1],
            edge[2, 7:8, :], edge[3, 7:8, :], edge[4, 0:1, :], edge[5, 0:1, :], edge[2, 0:4, :],
        ],
        axis=0,
    )
    rim = project(rim, w_in[:, :width])
    has_n = (my_y > 0).astype(F32)
    has_s = (my_y < ny - 1).astype(F32)
    has_w = (my_x > 0).astype(F32)
    has_e = (my_x < nx - 1).astype(F32)
    padded[0, 8 : 8 + COLS, :] = rim[0:16] * has_n
    padded[1 + ROWS, 8 : 8 + COLS, :] = rim[16:32] * has_s
    for r in range(ROWS):
        padded[1 + r, 7:8, :] = rim[32 + r : 33 + r] * has_w
        padded[1 + r, 8 + COLS : 9 + COLS, :] = rim[40 + r : 41 + r] * has_e
    padded[0, 7:8, :] = rim[48:49] * (has_n * has_w)
    padded[0, 8 + COLS : 9 + COLS, :] = rim[49:50] * (has_n * has_e)
    padded[1 + ROWS, 7:8, :] = rim[50:51] * (has_s * has_w)
    padded[1 + ROWS, 8 + COLS : 9 + COLS, :] = rim[51:52] * (has_s * has_e)

    def row_copy(member):
        return copy(row_out.at[member], row_in.at[member_x], row_send.at[member], row_recv.at[member_x], in_row(member))

    def col_copy(member):
        return copy(col_out.at[member], col_in.at[member_y], col_send.at[member], col_recv.at[member_y], in_col(member))

    def conv_row(r, carry):
        total = jnp.broadcast_to(conv_bias[...], (COLS, width))
        for i in range(3):
            for j in range(3):
                tap = 3 * i + j
                total = total + padded[r + i, 7 + j : 7 + j + COLS, :] * taps[tap : tap + 1, :]
        value = silu(total).astype(BF16)
        row_out[r] = value
        for g in range(groups):
            conved[g, pl.ds(pl.multiple_of(r * COLS, COLS), COLS), :] = value[:, g * LANES : (g + 1) * LANES].astype(F32)

        @pl.when(r != member_x)
        def _():
            row_copy(r).start()

        return carry

    lax.fori_loop(0, ROWS, conv_row, 0)
    row_in[member_x] = row_out[member_x]
    for c in range(COLS):
        column = [conved[g, pl.ds(c, ROWS, stride=COLS), :] for g in range(groups)]
        for g in range(groups // 2):
            both = jnp.concatenate([column[g], column[g + groups // 2]], axis=0)
            col_out[c, :, g * LANES : (g + 1) * LANES] = both.astype(BF16)
    col_in[member_y] = col_out[member_y]

    def start_col(turn, carry):
        col_copy(lax.rem(member_y + turn, COLS)).start()
        return carry

    lax.fori_loop(1, COLS, start_col, 0)

    def split_columns(stacked):
        value = stacked.astype(F32)
        left, right = value[:, :ROWS, :], value[:, ROWS:, :]
        return jnp.concatenate([left.reshape(LINE, hw), right.reshape(LINE, hw)], axis=1)

    def prepare(cells, k):
        weight = w_xt[k]
        low = lax.dot_general(cells, weight, (((1,), (1,)), ((), ())), preferred_element_type=F32)
        maps = lax.dot_general(weight, cells, (((1,), (1,)), ((), ())), preferred_element_type=F32)
        low = low[:, :24].astype(BF16)
        step = softplus(jnp.dot(low, w_dt[k], preferred_element_type=F32) + dt_bias[pl.ds(k, 1), :])
        push = step * cells.astype(F32)
        for g in range(groups):
            steps[g, :LINE] = step[:, g * LANES : (g + 1) * LANES]
            drive[g, :LINE] = push[:, g * LANES : (g + 1) * LANES]
        ins, outs = maps[24:32], maps[32:40]

        def spread(block, carry):
            shift = lax.rem(LINE - 8 * block, LINE)
            ins_here, outs_here = pltpu.roll(ins, shift, 1), pltpu.roll(outs, shift, 1)
            for i in range(8):
                in_map[8 * block + i] = jnp.broadcast_to(ins_here[:, i : i + 1], (8, LANES))
                out_map[8 * block + i] = jnp.broadcast_to(outs_here[:, i : i + 1], (8, LANES))
            return carry

        lax.fori_loop(0, LINE // 8, spread, 0)

    sub = lax.broadcasted_iota(jnp.int32, (8, LANES), 0)

    def scan(k, backward, start, total, first):
        rates = -jnp.exp(a_log[k]) * LOG2E
        masks = [lax.rem(sub // s, 2) == backward for s in (1, 2, 4)]

        def chunk(turn, state):
            base = pl.multiple_of((turn + backward * (LINE // 8 - 1 - 2 * turn)) * 8, 8)
            cell = [base + i + backward * (7 - 2 * i) for i in range(8)]
            state = list(state)
            for g in range(width // LANES):
                lanes = slice(g * LANES, (g + 1) * LANES)
                parts = []
                for i in range(8):
                    step = steps[g, pl.ds(cell[i], 8, stride=0), :]
                    push = drive[g, pl.ds(cell[i], 8, stride=0), :]
                    state[g] = jnp.exp2(step * rates[:, lanes]) * state[g] + in_map[cell[i]] * push
                    parts.append(out_map[cell[i]] * state[g])
                for s, mask in zip((1, 2, 4), masks):
                    parts = [
                        jnp.where(mask, a, b) + pltpu.roll(jnp.where(mask, b, a), s, 0)
                        for a, b in zip(parts[0::2], parts[1::2])
                    ]
                here = (pl.ds(base, 8), lanes)
                total[here] = parts[0] if first else total[here] + parts[0]
            return tuple(state)

        return lax.fori_loop(0, LINE // 8, chunk, start)

    def split(state):
        return tuple(state[:, g * LANES : (g + 1) * LANES] for g in range(width // LANES))

    zero = tuple(jnp.zeros((8, LANES), F32) for _ in range(width // LANES))
    state_copies = [
        copy(state_out.at[0], state_in.at[0], state_send.at[0], state_recv.at[0], over_x),
        copy(state_out.at[1], state_in.at[1], state_send.at[1], state_recv.at[1], over_y),
    ]

    def wait_row(turn, carry):
        member = lax.rem(member_x + turn, ROWS)
        copy(row_out.at[member], row_in.at[member], row_send.at[member], row_recv.at[member], in_row(member)).wait_recv()
        return carry

    def wait_col(turn, carry):
        member = lax.rem(member_y + turn, COLS)
        copy(col_out.at[member], col_in.at[member], col_send.at[member], col_recv.at[member], in_col(member)).wait_recv()
        return carry

    def send_state(index, state):
        for g in range(width // LANES):
            state_out[index, :, g * LANES : (g + 1) * LANES] = state[g]
        state_copies[index].start()

    lax.fori_loop(1, ROWS, wait_row, 0)
    row_cells = row_in[...].reshape(LINE, width)
    prepare(row_cells, half_x)
    send_state(0, scan(half_x, half_x, zero, row_sum, True))

    lax.fori_loop(1, COLS, wait_col, 0)
    col_cells = split_columns(col_in[...]).astype(BF16)
    prepare(col_cells, 2 + half_y)
    send_state(1, scan(2 + half_y, half_y, zero, col_sum, True))

    prepare(row_cells, 1 - half_x)
    state_copies[0].wait_recv()
    scan(1 - half_x, 1 - half_x, split(state_in[0]), row_sum, False)
    row_back_out[...] = row_sum[...].astype(BF16).reshape(ROWS, COLS, width)
    row_back_in[member_x] = row_back_out[member_x]

    def row_back(member, slot):
        return copy(row_back_out.at[member], row_back_in.at[slot], row_back_send.at[member], row_back_recv.at[slot], in_row(member))

    def col_back(member, slot):
        return copy(col_back_out.at[member], col_back_in.at[slot], col_back_send.at[member], col_back_recv.at[slot], in_col(member))

    def start_row_back(turn, carry):
        row_back(lax.rem(member_x + turn, ROWS), member_x).start()
        return carry

    lax.fori_loop(1, ROWS, start_row_back, 0)

    prepare(col_cells, 3 - half_y)
    state_copies[1].wait_recv()
    scan(3 - half_y, 1 - half_y, split(state_in[1]), col_sum, False)
    col_value = col_sum[...].reshape(COLS, ROWS, width)
    col_back_out[...] = jnp.concatenate([col_value[:, :, :hw], col_value[:, :, hw:]], axis=1).astype(BF16)
    col_back_in[member_y] = col_back_out[member_y]

    def start_col_back(turn, carry):
        col_back(lax.rem(member_y + turn, COLS), member_y).start()
        return carry

    lax.fori_loop(1, COLS, start_col_back, 0)

    def wait_row_back(turn, carry):
        member = lax.rem(member_x + turn, ROWS)
        row_back(member, member).wait_recv()
        return carry

    def wait_col_back(turn, carry):
        member = lax.rem(member_y + turn, COLS)
        col_back(member, member).wait_recv()
        return carry

    lax.fori_loop(1, ROWS, wait_row_back, 0)
    skip = jnp.sum(d_skip[...], axis=0, keepdims=True)
    row_value = row_back_in[...].reshape(LINE, width).astype(F32)
    for g in range(groups):
        lanes = slice(g * LANES, (g + 1) * LANES)
        summed[g, :LINE] = row_value[:, lanes] + skip[:, lanes] * conved[g, :LINE]
    lax.fori_loop(1, COLS, wait_col_back, 0)
    for c in range(COLS):
        value = col_back_in[c].astype(F32)
        for g in range(groups):
            here = (g, pl.ds(c, ROWS, stride=COLS), slice(None))
            low, high = (0, ROWS) if g < groups // 2 else (ROWS, 2 * ROWS)
            lane = (g % (groups // 2)) * LANES
            summed[here] = summed[here] + value[low:high, lane : lane + LANES]
    total = jnp.concatenate([summed[g, :LINE] for g in range(groups)], axis=1)
    gated = (unit_norm(total) * out_gain[...] + out_bias[...]) * silu(gate[...])
    mixed = tokens[...].astype(F32).reshape(ROWS * COLS, -1) + jnp.dot(gated.astype(BF16), w_out[...], preferred_element_type=F32)
    out[...] = mixed.reshape(out.shape).astype(BF16)

    for item in edges + state_copies:
        item.wait_send()

    def drain_row(turn, carry):
        member = lax.rem(member_x + turn, ROWS)
        row_copy(member).wait_send()
        row_back(member, member_x).wait_send()
        return carry

    def drain_col(turn, carry):
        member = lax.rem(member_y + turn, COLS)
        col_copy(member).wait_send()
        col_back(member, member_y).wait_send()
        return carry

    lax.fori_loop(1, ROWS, drain_row, 0)
    lax.fori_loop(1, COLS, drain_col, 0)


def shards(tokens, norm_gain, norm_bias, w_in, conv_taps, conv_bias, w_x, w_dt, dt_bias, a_log, d_skip, out_gain, out_bias, w_out):
    chans, width = tokens.shape[-1], w_out.shape[0]
    hw = width // 2
    dma = pltpu.SemaphoreType.DMA
    vmem = pl.BlockSpec(memory_space=pltpu.VMEM)
    return pl.pallas_call(
        kernel,
        out_shape=jax.ShapeDtypeStruct(tokens.shape, tokens.dtype),
        in_specs=[vmem] * 14,
        out_specs=vmem,
        scratch_shapes=[
            pltpu.VMEM((6, ROWS, chans), F32),
            pltpu.VMEM((2, COLS, chans), BF16),
            pltpu.VMEM((2, ROWS, chans), F32),
            pltpu.VMEM((2, COLS, chans), BF16),
            pltpu.VMEM((ROWS + 2, COLS + 16, width), F32),
            pltpu.VMEM((width // LANES, LINE + COLS, LANES), F32),
            pltpu.VMEM((width // LANES, LINE + COLS, LANES), F32),
            pltpu.VMEM((ROWS * COLS, width), F32),
            pltpu.VMEM((ROWS, COLS, width), BF16),
            pltpu.VMEM((COLS, 2 * ROWS, hw), BF16),
            pltpu.VMEM((ROWS, COLS, width), BF16),
            pltpu.VMEM((COLS, 2 * ROWS, hw), BF16),
            pltpu.VMEM((width // LANES, LINE + 8, LANES), F32),
            pltpu.VMEM((width // LANES, LINE + 8, LANES), F32),
            pltpu.VMEM((LINE, 8, LANES), F32),
            pltpu.VMEM((LINE, 8, LANES), F32),
            pltpu.VMEM((LINE, width), F32),
            pltpu.VMEM((LINE, width), F32),
            pltpu.VMEM((2, 8, width), F32),
            pltpu.VMEM((2, 8, width), F32),
            pltpu.VMEM((ROWS, COLS, width), BF16),
            pltpu.VMEM((COLS, 2 * ROWS, hw), BF16),
            pltpu.VMEM((ROWS, COLS, width), BF16),
            pltpu.VMEM((COLS, 2 * ROWS, hw), BF16),
            dma((8,)), dma((8,)), dma((ROWS,)), dma((ROWS,)), dma((COLS,)), dma((COLS,)), dma((2,)), dma((2,)),
            dma((ROWS,)), dma((ROWS,)), dma((COLS,)), dma((COLS,)),
        ],
        compiler_params=pltpu.CompilerParams(collective_id=0, has_side_effects=True, vmem_limit_bytes=40 * 1024 * 1024),
    )(
        tokens, norm_gain.reshape(1, -1), norm_bias.reshape(1, -1), w_in, conv_taps, conv_bias.reshape(1, -1),
        jnp.transpose(w_x, (0, 2, 1)), w_dt, dt_bias, a_log, d_skip, out_gain.reshape(1, -1), out_bias.reshape(1, -1), w_out,
    )


def solution(mesh):
    placed = (P("gy", "gx", None),) + (P(),) * 13
    return jax.shard_map(shards, mesh=mesh, in_specs=placed, out_specs=P("gy", "gx", None), check_vma=False)
```

```python
import functools

import jax
import jax.numpy as jnp
from jax import lax
from jax.experimental import pallas as pl
from jax.experimental.pallas import tpu as pltpu
from jax.sharding import PartitionSpec as P

MESH = pl.DeviceIdType.MESH
F32 = jnp.float32
BF16 = jnp.bfloat16
LOG2E = 1.4426950408889634
ROWS, COLS = 8, 16
LINE = 128
LANES = 128


def rounded(value):
    return value.astype(BF16).astype(F32)


def unit_norm(values):
    mean = jnp.mean(values, axis=-1, keepdims=True)
    centred = values - mean
    spread = jnp.mean(centred * centred, axis=-1, keepdims=True)
    return centred * lax.rsqrt(spread + 1e-05)


def softplus(value):
    return jnp.maximum(value, 0.0) + jnp.log1p(jnp.exp(-jnp.abs(value)))


def silu(value):
    return value / (1.0 + jnp.exp(-value))


def kernel(
    tokens_hbm, w_in_hbm, norm_gain_hbm, norm_bias_hbm, taps_hbm, conv_bias_hbm, w_xt_hbm, w_dt_hbm, dt_bias_hbm, a_log_hbm,
    d_skip_hbm, out_gain_hbm, out_bias_hbm, w_out_hbm,
    out,
    tokens, w_in, norm_gain, norm_bias, taps, conv_bias, w_xt, w_dt, dt_bias, a_log, d_skip, out_gain, out_bias, w_out,
    load_sem,
    edge, edge_row, edge_col, halo, padded, conved, summed, gate, row_out, col_out, row_in, col_in,
    cell_maps, steps, drive, in_map, out_map, row_sum, col_sum, state_out, state_in,
    row_back_out, col_back_out, row_back_in, col_back_in,
    edge_send, edge_recv, row_send, row_recv, col_send, col_recv, state_send, state_recv,
    row_back_send, row_back_recv, col_back_send, col_back_recv,
):
    ny, nx = lax.axis_size("gy"), lax.axis_size("gx")
    my_y, my_x = lax.axis_index("gy"), lax.axis_index("gx")
    half_x, member_x = my_x // ROWS, lax.rem(my_x, ROWS)
    member_y = lax.rem(my_y, COLS)
    half_y = lax.rem(my_x, 2)
    own_col = (my_y // COLS == half_y).astype(jnp.int32)
    north, south = lax.rem(my_y + ny - 1, ny), lax.rem(my_y + 1, ny)
    west, east = lax.rem(my_x + nx - 1, nx), lax.rem(my_x + 1, nx)
    over_x = (my_y, lax.rem(my_x + ROWS, nx))
    over_y = (my_y, my_x + 1 - 2 * half_y)
    around = [(north, my_x), (south, my_x), (my_y, west), (my_y, east), (north, west), (north, east), (south, west), (south, east)]

    def in_row(member):
        return (my_y, half_x * ROWS + member)

    def in_col(member):
        return (half_y * COLS + member, my_x - half_y + my_y // COLS)

    pairs = [
        (tokens_hbm, tokens), (w_in_hbm, w_in), (norm_gain_hbm, norm_gain), (norm_bias_hbm, norm_bias), (taps_hbm, taps),
        (conv_bias_hbm, conv_bias), (w_xt_hbm, w_xt), (w_dt_hbm, w_dt), (dt_bias_hbm, dt_bias), (a_log_hbm, a_log),
        (d_skip_hbm, d_skip), (out_gain_hbm, out_gain), (out_bias_hbm, out_bias), (w_out_hbm, w_out),
    ]
    loads = [pltpu.make_async_copy(src, dst, load_sem.at[i]) for i, (src, dst) in enumerate(pairs)]
    for item in loads:
        item.start()

    barrier = pltpu.get_barrier_semaphore()

    def greet(device):
        pl.semaphore_signal(barrier, inc=1, device_id=device, device_id_type=MESH)

    for device in around + [over_x, over_y]:
        greet(device)

    def greet_row(turn, carry):
        greet(in_row(lax.rem(member_x + turn, ROWS)))
        return carry

    def greet_col(turn, carry):
        greet(in_col(lax.rem(member_y + turn, COLS)))
        return carry

    lax.fori_loop(1, ROWS, greet_row, 0)
    lax.fori_loop(own_col, COLS, greet_col, 0)

    def copy(src, dst, send, recv, device):
        return pltpu.make_async_remote_copy(
            src_ref=src, dst_ref=dst, send_sem=send, recv_sem=recv, device_id=device, device_id_type=MESH
        )

    loads[0].wait()
    token_float = tokens[...].astype(F32)
    for r in range(ROWS):
        edge_col[0, r : r + 1, :] = token_float[r, 0:1, :]
        edge_col[1, r : r + 1, :] = token_float[r, COLS - 1 : COLS, :]
    edge_row[0] = tokens[0]
    edge_row[1] = tokens[ROWS - 1]
    pl.semaphore_wait(barrier, 10 + ROWS - 1 + COLS - own_col)
    sends = [
        (edge_row.at[0], halo.at[1], 1, around[0]),
        (edge_row.at[1], halo.at[0], 0, around[1]),
        (edge_col.at[0], edge.at[1], 3, around[2]),
        (edge_col.at[1], edge.at[0], 2, around[3]),
        (edge_col.at[0], edge.at[5], 7, around[4]),
        (edge_col.at[1], edge.at[4], 6, around[5]),
        (edge_col.at[0], edge.at[3], 5, around[6]),
        (edge_col.at[1], edge.at[2], 4, around[7]),
    ]
    edges = [copy(src, dst, edge_send.at[slot], edge_recv.at[slot], device) for src, dst, slot, device in sends]
    for item in edges:
        item.start()

    for item in loads[1:]:
        item.wait()
    gain, bias = norm_gain[...].reshape(1, -1), norm_bias[...].reshape(1, -1)

    def project(cells, weight):
        normed = (unit_norm(cells) * gain + bias).astype(BF16)
        return rounded(jnp.dot(normed, weight, preferred_element_type=F32))

    cells = token_float.reshape(ROWS * COLS, -1)
    normed = (unit_norm(cells) * gain + bias).astype(BF16)
    width = gate.shape[1]
    hw, groups = width // 2, width // LANES
    inner = rounded(jnp.dot(normed, w_in[:, :width], preferred_element_type=F32))
    padded[1 : 1 + ROWS, 8 : 8 + COLS, :] = inner.reshape(ROWS, COLS, width)
    gate[...] = rounded(jnp.dot(normed, w_in[:, width:], preferred_element_type=F32))

    for item in edges:
        item.wait_recv()
    rim = jnp.concatenate(
        [
            halo[0].astype(F32), halo[1].astype(F32), edge[0], edge[1],
            edge[2, 7:8, :], edge[3, 7:8, :], edge[4, 0:1, :], edge[5, 0:1, :], edge[2, 0:4, :],
        ],
        axis=0,
    )
    rim = project(rim, w_in[:, :width])
    has_n = (my_y > 0).astype(F32)
    has_s = (my_y < ny - 1).astype(F32)
    has_w = (my_x > 0).astype(F32)
    has_e = (my_x < nx - 1).astype(F32)
    padded[0, 8 : 8 + COLS, :] = rim[0:16] * has_n
    padded[1 + ROWS, 8 : 8 + COLS, :] = rim[16:32] * has_s
    for r in range(ROWS):
        padded[1 + r, 7:8, :] = rim[32 + r : 33 + r] * has_w
        padded[1 + r, 8 + COLS : 9 + COLS, :] = rim[40 + r : 41 + r] * has_e
    padded[0, 7:8, :] = rim[48:49] * (has_n * has_w)
    padded[0, 8 + COLS : 9 + COLS, :] = rim[49:50] * (has_n * has_e)
    padded[1 + ROWS, 7:8, :] = rim[50:51] * (has_s * has_w)
    padded[1 + ROWS, 8 + COLS : 9 + COLS, :] = rim[51:52] * (has_s * has_e)

    def row_copy(member):
        return copy(row_out.at[member], row_in.at[member_x], row_send.at[member], row_recv.at[member_x], in_row(member))

    def col_copy(member):
        return copy(col_out.at[member], col_in.at[member_y], col_send.at[member], col_recv.at[member_y], in_col(member))

    def conv_row(r, carry):
        total = jnp.broadcast_to(conv_bias[...].reshape(1, -1), (COLS, width))
        for i in range(3):
            for j in range(3):
                tap = 3 * i + j
                total = total + padded[r + i, 7 + j : 7 + j + COLS, :] * taps[tap : tap + 1, :]
        value = silu(total).astype(BF16)
        row_out[r] = value
        for g in range(groups):
            conved[g, pl.ds(pl.multiple_of(r * COLS, COLS), COLS), :] = value[:, g * LANES : (g + 1) * LANES].astype(F32)

        @pl.when(r != member_x)
        def _():
            row_copy(r).start()

        return carry

    lax.fori_loop(0, ROWS, conv_row, 0)
    row_in[member_x] = row_out[member_x]
    for c in range(COLS):
        column = [conved[g, pl.ds(c, ROWS, stride=COLS), :] for g in range(groups)]
        for g in range(groups // 2):
            both = jnp.concatenate([column[g], column[g + groups // 2]], axis=0)
            col_out[c, :, g * LANES : (g + 1) * LANES] = both.astype(BF16)

    @pl.when(own_col == 1)
    def _():
        col_in[member_y] = col_out[member_y]

    def start_col(turn, carry):
        col_copy(lax.rem(member_y + turn, COLS)).start()
        return carry

    lax.fori_loop(own_col, COLS, start_col, 0)

    def split_columns(stacked):
        value = stacked.astype(F32)
        left, right = value[:, :ROWS, :], value[:, ROWS:, :]
        return jnp.concatenate([left.reshape(LINE, hw), right.reshape(LINE, hw)], axis=1)

    eighth = lax.broadcasted_iota(jnp.int32, (LANES, 4 * LANES), 0) // 8
    block = lax.broadcasted_iota(jnp.int32, (LANES, 4 * LANES), 1) // LANES
    pick = ((eighth == block + jnp.where(block < 2, 3, 6)) | (eighth == block + 10)).astype(F32).astype(BF16)
    lane = lax.broadcasted_iota(jnp.int32, (8, LANES), 1)
    own_state = lane % 8 == lax.broadcasted_iota(jnp.int32, (8, LANES), 0)

    def prepare(cells, first):
        weight = w_xt[40 * first : 40 * first + 80, :]
        proj = lax.dot_general(cells, weight, (((1,), (1,)), ((), ())), preferred_element_type=F32)
        cells_float = cells.astype(F32)
        ranks = w_dt[...].astype(F32)
        for side in range(2):
            k = first + side
            low = proj[:, 40 * side : 40 * side + 24].astype(BF16)
            rank = ranks[24 * k : 24 * k + 24].astype(BF16)
            step = softplus(jnp.dot(low, rank, preferred_element_type=F32) + dt_bias[k : k + 1, :])
            push = step * cells_float
            for g in range(groups):
                steps[k, g, :LINE] = step[:, g * LANES : (g + 1) * LANES]
                drive[k, g, :LINE] = push[:, g * LANES : (g + 1) * LANES]
        proj = jnp.concatenate([proj, jnp.zeros((LINE, LANES - 80), F32)], axis=1)
        high = rounded(proj)
        left = rounded(proj - high)
        wide = lax.broadcasted_iota(jnp.int32, (LINE, LANES), 1)
        cell_maps[:LINE] = jnp.where(wide < 80, high, jnp.where(wide < 96, pltpu.roll(left, 56, 1), pltpu.roll(left, 32, 1)))
        rows = [jnp.where(own_state, cell_maps[pl.ds(cell, 8, stride=0), :], 0.0) for cell in range(LINE)]
        maps = jnp.dot(jnp.concatenate(rows, axis=0).astype(BF16), pick, preferred_element_type=F32)
        maps = maps.reshape(LINE, 8, 4 * LANES)
        for side in range(2):
            in_map[first + side] = maps[:, :, 2 * side * LANES : (2 * side + 1) * LANES]
            out_map[first + side] = maps[:, :, (2 * side + 1) * LANES : (2 * side + 2) * LANES]

    sub = lax.broadcasted_iota(jnp.int32, (8, LANES), 0)

    def scan(k, backward, start, total, first):
        rates = -jnp.exp(a_log[k]) * LOG2E
        masks = [lax.rem(sub // s, 2) == backward for s in (1, 2, 4)]

        def chunk(turn, state):
            base = pl.multiple_of((turn + backward * (LINE // 8 - 1 - 2 * turn)) * 8, 8)
            cell = [base + i + backward * (7 - 2 * i) for i in range(8)]
            state = list(state)
            for g in range(width // LANES):
                lanes = slice(g * LANES, (g + 1) * LANES)
                parts = []
                for i in range(8):
                    step = steps[k, g, pl.ds(cell[i], 8, stride=0), :]
                    push = drive[k, g, pl.ds(cell[i], 8, stride=0), :]
                    state[g] = jnp.exp2(step * rates[:, lanes]) * state[g] + in_map[k, cell[i]] * push
                    parts.append(out_map[k, cell[i]] * state[g])
                for s, mask in zip((1, 2, 4), masks):
                    parts = [
                        jnp.where(mask, a, b) + pltpu.roll(jnp.where(mask, b, a), s, 0)
                        for a, b in zip(parts[0::2], parts[1::2])
                    ]
                here = (pl.ds(base, 8), lanes)
                total[here] = parts[0] if first else total[here] + parts[0]
            return tuple(state)

        return lax.fori_loop(0, LINE // 8, chunk, start)

    def split(state):
        return tuple(state[:, g * LANES : (g + 1) * LANES] for g in range(width // LANES))

    zero = tuple(jnp.zeros((8, LANES), F32) for _ in range(width // LANES))
    state_copies = [
        copy(state_out.at[0], state_in.at[0], state_send.at[0], state_recv.at[0], over_x),
        copy(state_out.at[1], state_in.at[1], state_send.at[1], state_recv.at[1], over_y),
    ]

    def wait_row(turn, carry):
        member = lax.rem(member_x + turn, ROWS)
        copy(row_out.at[member], row_in.at[member], row_send.at[member], row_recv.at[member], in_row(member)).wait_recv()
        return carry

    def wait_col(turn, carry):
        member = lax.rem(member_y + turn, COLS)
        copy(col_out.at[member], col_in.at[member], col_send.at[member], col_recv.at[member], in_col(member)).wait_recv()
        return carry

    def send_state(index, state):
        for g in range(width // LANES):
            state_out[index, :, g * LANES : (g + 1) * LANES] = state[g]
        state_copies[index].start()

    lax.fori_loop(1, ROWS, wait_row, 0)
    row_cells = row_in[...].reshape(LINE, width)
    prepare(row_cells, 0)
    send_state(0, scan(half_x, half_x, zero, row_sum, True))

    lax.fori_loop(own_col, COLS, wait_col, 0)
    col_cells = split_columns(col_in[...]).astype(BF16)
    prepare(col_cells, 2)
    send_state(1, scan(2 + half_y, half_y, zero, col_sum, True))

    state_copies[0].wait_recv()
    scan(1 - half_x, 1 - half_x, split(state_in[0]), row_sum, False)
    row_back_out[...] = row_sum[...].astype(BF16).reshape(ROWS, COLS, width)
    row_back_in[member_x] = row_back_out[member_x]

    def row_back(member, slot):
        return copy(row_back_out.at[member], row_back_in.at[slot], row_back_send.at[member], row_back_recv.at[slot], in_row(member))

    def col_back(member, slot):
        return copy(col_back_out.at[member], col_back_in.at[slot], col_back_send.at[member], col_back_recv.at[slot], in_col(member))

    def start_row_back(turn, carry):
        row_back(lax.rem(member_x + turn, ROWS), member_x).start()
        return carry

    lax.fori_loop(1, ROWS, start_row_back, 0)

    state_copies[1].wait_recv()
    scan(3 - half_y, 1 - half_y, split(state_in[1]), col_sum, False)
    col_value = col_sum[...].reshape(COLS, ROWS, width)
    col_back_out[...] = jnp.concatenate([col_value[:, :, :hw], col_value[:, :, hw:]], axis=1).astype(BF16)

    @pl.when(own_col == 1)
    def _():
        col_back_in[member_y] = col_back_out[member_y]

    def start_col_back(turn, carry):
        col_back(lax.rem(member_y + turn, COLS), member_y).start()
        return carry

    lax.fori_loop(own_col, COLS, start_col_back, 0)

    def wait_row_back(turn, carry):
        member = lax.rem(member_x + turn, ROWS)
        row_back(member, member).wait_recv()
        return carry

    def wait_col_back(turn, carry):
        member = lax.rem(member_y + turn, COLS)
        col_back(member, member).wait_recv()
        return carry

    lax.fori_loop(1, ROWS, wait_row_back, 0)
    skip = jnp.sum(d_skip[...], axis=0, keepdims=True)
    row_value = row_back_in[...].reshape(LINE, width).astype(F32)
    for g in range(groups):
        lanes = slice(g * LANES, (g + 1) * LANES)
        summed[g, :LINE] = row_value[:, lanes] + skip[:, lanes] * conved[g, :LINE]
    lax.fori_loop(own_col, COLS, wait_col_back, 0)
    for c in range(COLS):
        value = col_back_in[c].astype(F32)
        for g in range(groups):
            here = (g, pl.ds(c, ROWS, stride=COLS), slice(None))
            low, high = (0, ROWS) if g < groups // 2 else (ROWS, 2 * ROWS)
            lane = (g % (groups // 2)) * LANES
            summed[here] = summed[here] + value[low:high, lane : lane + LANES]
    total = jnp.concatenate([summed[g, :LINE] for g in range(groups)], axis=1)
    gated = (unit_norm(total) * out_gain[...].reshape(1, -1) + out_bias[...].reshape(1, -1)) * silu(gate[...])
    mixed = tokens[...].astype(F32).reshape(ROWS * COLS, -1) + jnp.dot(gated.astype(BF16), w_out[...], preferred_element_type=F32)
    out[...] = mixed.reshape(out.shape).astype(BF16)

    for item in edges + state_copies:
        item.wait_send()

    def drain_row(turn, carry):
        member = lax.rem(member_x + turn, ROWS)
        row_copy(member).wait_send()
        row_back(member, member_x).wait_send()
        return carry

    def drain_col(turn, carry):
        member = lax.rem(member_y + turn, COLS)
        col_copy(member).wait_send()
        col_back(member, member_y).wait_send()
        return carry

    lax.fori_loop(1, ROWS, drain_row, 0)
    lax.fori_loop(own_col, COLS, drain_col, 0)


def shards(tokens, norm_gain, norm_bias, w_in, conv_taps, conv_bias, w_x, w_dt, dt_bias, a_log, d_skip, out_gain, out_bias, w_out):
    chans, width = tokens.shape[-1], w_out.shape[0]
    hw = width // 2
    dma = pltpu.SemaphoreType.DMA
    operands = (
        tokens, w_in, norm_gain, norm_bias, conv_taps, conv_bias, jnp.transpose(w_x, (0, 2, 1)).reshape(-1, width),
        w_dt.reshape(-1, width), dt_bias, a_log, d_skip, out_gain, out_bias, w_out,
    )
    return pl.pallas_call(
        kernel,
        out_shape=jax.ShapeDtypeStruct(tokens.shape, tokens.dtype),
        in_specs=[pl.BlockSpec(memory_space=pltpu.MemorySpace.HBM)] * 14,
        out_specs=pl.BlockSpec(memory_space=pltpu.VMEM),
        scratch_shapes=[pltpu.VMEM(value.shape, value.dtype) for value in operands] + [
            dma((14,)),
            pltpu.VMEM((6, ROWS, chans), F32),
            pltpu.VMEM((2, COLS, chans), BF16),
            pltpu.VMEM((2, ROWS, chans), F32),
            pltpu.VMEM((2, COLS, chans), BF16),
            pltpu.VMEM((ROWS + 2, COLS + 16, width), F32),
            pltpu.VMEM((width // LANES, LINE + COLS, LANES), F32),
            pltpu.VMEM((width // LANES, LINE + COLS, LANES), F32),
            pltpu.VMEM((ROWS * COLS, width), F32),
            pltpu.VMEM((ROWS, COLS, width), BF16),
            pltpu.VMEM((COLS, 2 * ROWS, hw), BF16),
            pltpu.VMEM((ROWS, COLS, width), BF16),
            pltpu.VMEM((COLS, 2 * ROWS, hw), BF16),
            pltpu.VMEM((LINE + 8, LANES), F32),
            pltpu.VMEM((4, width // LANES, LINE + 8, LANES), F32),
            pltpu.VMEM((4, width // LANES, LINE + 8, LANES), F32),
            pltpu.VMEM((4, LINE, 8, LANES), F32),
            pltpu.VMEM((4, LINE, 8, LANES), F32),
            pltpu.VMEM((LINE, width), F32),
            pltpu.VMEM((LINE, width), F32),
            pltpu.VMEM((2, 8, width), F32),
            pltpu.VMEM((2, 8, width), F32),
            pltpu.VMEM((ROWS, COLS, width), BF16),
            pltpu.VMEM((COLS, 2 * ROWS, hw), BF16),
            pltpu.VMEM((ROWS, COLS, width), BF16),
            pltpu.VMEM((COLS, 2 * ROWS, hw), BF16),
            dma((8,)), dma((8,)), dma((ROWS,)), dma((ROWS,)), dma((COLS,)), dma((COLS,)), dma((2,)), dma((2,)),
            dma((ROWS,)), dma((ROWS,)), dma((COLS,)), dma((COLS,)),
        ],
        compiler_params=pltpu.CompilerParams(collective_id=0, has_side_effects=True, vmem_limit_bytes=60 * 1024 * 1024),
    )(*operands)


def solution(mesh):
    placed = (P("gy", "gx", None),) + (P(),) * 13
    return jax.shard_map(shards, mesh=mesh, in_specs=placed, out_specs=P("gy", "gx", None), check_vma=False)
```

```python
import functools

import jax
import jax.numpy as jnp
from jax import lax
from jax.experimental import pallas as pl
from jax.experimental.pallas import tpu as pltpu
from jax.sharding import PartitionSpec as P

MESH = pl.DeviceIdType.MESH
F32 = jnp.float32
BF16 = jnp.bfloat16
LOG2E = 1.4426950408889634
ROWS, COLS = 8, 16
LINE = 128
LANES = 128


def rounded(value):
    return value.astype(BF16).astype(F32)


def unit_norm(values):
    mean = jnp.mean(values, axis=-1, keepdims=True)
    centred = values - mean
    spread = jnp.mean(centred * centred, axis=-1, keepdims=True)
    return centred * lax.rsqrt(spread + 1e-05)


def softplus(value):
    return jnp.maximum(value, 0.0) + jnp.log1p(jnp.exp(-jnp.abs(value)))


def silu(value):
    return value / (1.0 + jnp.exp(-value))


def kernel(
    tokens_hbm, w_in_hbm, norm_gain_hbm, norm_bias_hbm, taps_hbm, conv_bias_hbm, w_xt_hbm, w_dt_hbm, dt_bias_hbm, a_log_hbm,
    d_skip_hbm, out_gain_hbm, out_bias_hbm, w_out_hbm,
    out,
    tokens, w_in, norm_gain, norm_bias, taps, conv_bias, w_xt, w_dt, dt_bias, a_log, d_skip, out_gain, out_bias, w_out,
    load_sem,
    edge, edge_row, edge_col, halo, padded, beside, conved, summed, gate, row_out, col_out, row_in, col_in,
    cell_maps, steps, drive, in_map, out_map, row_sum, col_sum, state_out, state_in,
    row_back_out, col_back_out, row_back_in, col_back_in,
    edge_send, edge_recv, row_send, row_recv, col_send, col_recv, state_send, state_recv,
    row_back_send, row_back_recv, col_back_send, col_back_recv,
):
    ny, nx = lax.axis_size("gy"), lax.axis_size("gx")
    my_y, my_x = lax.axis_index("gy"), lax.axis_index("gx")
    half_x, member_x = my_x // ROWS, lax.rem(my_x, ROWS)
    member_y = lax.rem(my_y, COLS)
    half_y = lax.rem(my_x, 2)
    own_col = (my_y // COLS == half_y).astype(jnp.int32)
    north, south = lax.rem(my_y + ny - 1, ny), lax.rem(my_y + 1, ny)
    west, east = lax.rem(my_x + nx - 1, nx), lax.rem(my_x + 1, nx)
    over_x = (my_y, lax.rem(my_x + ROWS, nx))
    over_y = (my_y, my_x + 1 - 2 * half_y)
    around = [(north, my_x), (south, my_x), (my_y, west), (my_y, east), (north, west), (north, east), (south, west), (south, east)]

    def in_row(member):
        return (my_y, half_x * ROWS + member)

    def in_col(member):
        return (half_y * COLS + member, my_x - half_y + my_y // COLS)

    pairs = [
        (tokens_hbm, tokens), (w_in_hbm, w_in), (norm_gain_hbm, norm_gain), (norm_bias_hbm, norm_bias), (taps_hbm, taps),
        (conv_bias_hbm, conv_bias), (w_xt_hbm, w_xt), (w_dt_hbm, w_dt), (dt_bias_hbm, dt_bias), (a_log_hbm, a_log),
        (d_skip_hbm, d_skip), (out_gain_hbm, out_gain), (out_bias_hbm, out_bias), (w_out_hbm, w_out),
    ]
    loads = [pltpu.make_async_copy(src, dst, load_sem.at[i]) for i, (src, dst) in enumerate(pairs)]
    loads[0].start()

    barrier = pltpu.get_barrier_semaphore()

    def greet(device):
        pl.semaphore_signal(barrier, inc=1, device_id=device, device_id_type=MESH)

    for device in around + [over_x, over_y]:
        greet(device)

    def greet_row(turn, carry):
        greet(in_row(lax.rem(member_x + turn, ROWS)))
        return carry

    def greet_col(turn, carry):
        greet(in_col(lax.rem(member_y + turn, COLS)))
        return carry

    lax.fori_loop(1, ROWS, greet_row, 0)
    lax.fori_loop(own_col, COLS, greet_col, 0)
    for item in loads[1:]:
        item.start()

    def copy(src, dst, send, recv, device):
        return pltpu.make_async_remote_copy(
            src_ref=src, dst_ref=dst, send_sem=send, recv_sem=recv, device_id=device, device_id_type=MESH
        )

    loads[0].wait()
    token_float = tokens[...].astype(F32)
    for r in range(ROWS):
        edge_col[0, r : r + 1, :] = token_float[r, 0:1, :]
        edge_col[1, r : r + 1, :] = token_float[r, COLS - 1 : COLS, :]
    edge_row[0] = tokens[0]
    edge_row[1] = tokens[ROWS - 1]
    pl.semaphore_wait(barrier, 10 + ROWS - 1 + COLS - own_col)
    sends = [
        (edge_row.at[0], halo.at[1], 1, around[0]),
        (edge_row.at[1], halo.at[0], 0, around[1]),
        (edge_col.at[0], edge.at[1], 3, around[2]),
        (edge_col.at[1], edge.at[0], 2, around[3]),
        (edge_col.at[0, pl.ds(0, 1)], edge.at[5, pl.ds(0, 1)], 7, around[4]),
        (edge_col.at[1, pl.ds(0, 1)], edge.at[4, pl.ds(0, 1)], 6, around[5]),
        (edge_col.at[0, pl.ds(7, 1)], edge.at[3, pl.ds(7, 1)], 5, around[6]),
        (edge_col.at[1, pl.ds(7, 1)], edge.at[2, pl.ds(7, 1)], 4, around[7]),
    ]
    edges = [copy(src, dst, edge_send.at[slot], edge_recv.at[slot], device) for src, dst, slot, device in sends]
    for item in edges:
        item.start()

    for item in loads[1:]:
        item.wait()
    gain, bias = norm_gain[...].reshape(1, -1), norm_bias[...].reshape(1, -1)

    def project(cells, weight):
        normed = (unit_norm(cells) * gain + bias).astype(BF16)
        return rounded(jnp.dot(normed, weight, preferred_element_type=F32))

    cells = token_float.reshape(ROWS * COLS, -1)
    normed = (unit_norm(cells) * gain + bias).astype(BF16)
    width = gate.shape[1]
    hw, groups = width // 2, width // LANES
    inner = rounded(jnp.dot(normed, w_in[:, :width], preferred_element_type=F32))
    padded[...] = jnp.zeros(padded.shape, F32)
    padded[1 : 1 + ROWS, 8 : 8 + COLS, :] = inner.reshape(ROWS, COLS, width)
    gate[...] = silu(rounded(jnp.dot(normed, w_in[:, width:], preferred_element_type=F32)))

    def conv_row(r, carry):
        total = jnp.broadcast_to(conv_bias[...].reshape(1, -1), (COLS, width))
        for i in range(3):
            for j in range(3):
                tap = 3 * i + j
                total = total + padded[r + i, 7 + j : 7 + j + COLS, :] * taps[tap : tap + 1, :]
        for g in range(groups):
            conved[g, pl.ds(pl.multiple_of(r * COLS, COLS), COLS), :] = total[:, g * LANES : (g + 1) * LANES]
        return carry

    lax.fori_loop(0, ROWS, conv_row, 0)
    for item in edges:
        item.wait_recv()
    rim = jnp.concatenate(
        [
            halo[0].astype(F32), halo[1].astype(F32), edge[0], edge[1],
            edge[2, 7:8, :], edge[3, 7:8, :], edge[4, 0:1, :], edge[5, 0:1, :], edge[0, 0:4, :],
        ],
        axis=0,
    )
    rim = project(rim, w_in[:, :width])
    has_n = (my_y > 0).astype(F32)
    has_s = (my_y < ny - 1).astype(F32)
    has_w = (my_x > 0).astype(F32)
    has_e = (my_x < nx - 1).astype(F32)
    beside[0, 8 : 8 + COLS, :] = rim[0:16] * has_n
    beside[0, 7:8, :] = rim[48:49] * (has_n * has_w)
    beside[0, 8 + COLS : 9 + COLS, :] = rim[49:50] * (has_n * has_e)
    beside[1, 8 : 8 + COLS, :] = rim[16:32] * has_s
    beside[1, 7:8, :] = rim[50:51] * (has_s * has_w)
    beside[1, 8 + COLS : 9 + COLS, :] = rim[51:52] * (has_s * has_e)
    nothing = jnp.zeros((8, width), F32)
    for side, value in ((2, rim[32:40] * has_w), (3, rim[40:48] * has_e)):
        beside[side, 0:8, :] = nothing
        beside[side, 8:16, :] = value
        beside[side, 16:24, :] = nothing
    for side, row in ((0, 0), (1, ROWS - 1)):
        more = sum(beside[side, 7 + j : 7 + j + COLS, :] * taps[6 * side + j : 6 * side + j + 1, :] for j in range(3))
        for g in range(groups):
            here = (g, slice(row * COLS, row * COLS + COLS))
            conved[here] = conved[here] + more[:, g * LANES : (g + 1) * LANES]
    for side, col in ((2, 0), (3, COLS - 1)):
        tap = 0 if side == 2 else 2
        more = sum(beside[side, 7 + i : 15 + i, :] * taps[3 * i + tap : 3 * i + tap + 1, :] for i in range(3))
        for g in range(groups):
            here = (g, pl.ds(col, ROWS, stride=COLS))
            conved[here] = conved[here] + more[:, g * LANES : (g + 1) * LANES]

    def row_copy(member):
        return copy(row_out.at[member], row_in.at[member_x], row_send.at[member], row_recv.at[member_x], in_row(member))

    def col_copy(member):
        return copy(col_out.at[member], col_in.at[member_y], col_send.at[member], col_recv.at[member_y], in_col(member))

    for r in range(ROWS):
        for g in range(groups):
            here = (g, slice(r * COLS, r * COLS + COLS))
            value = silu(conved[here]).astype(BF16)
            row_out[r, :, g * LANES : (g + 1) * LANES] = value
            conved[here] = value.astype(F32)
    for c in range(COLS):
        column = [conved[g, pl.ds(c, ROWS, stride=COLS), :] for g in range(groups)]
        for g in range(groups // 2):
            both = jnp.concatenate([column[g], column[g + groups // 2]], axis=0)
            col_out[c, :, g * LANES : (g + 1) * LANES] = both.astype(BF16)

    def start_col(turn, carry):
        col_copy(lax.rem(member_y + turn, COLS)).start()
        return carry

    def start_row(turn, carry):
        row_copy(lax.rem(member_x + turn, ROWS)).start()
        return carry

    lax.fori_loop(own_col, COLS, start_col, 0)
    lax.fori_loop(1, ROWS, start_row, 0)
    row_in[member_x] = row_out[member_x]

    @pl.when(own_col == 1)
    def _():
        col_in[member_y] = col_out[member_y]

    skip = jnp.sum(d_skip[...], axis=0, keepdims=True)
    for g in range(groups):
        summed[g, :LINE] = skip[:, g * LANES : (g + 1) * LANES] * conved[g, :LINE]

    def split_columns(stacked):
        value = stacked.astype(F32)
        left, right = value[:, :ROWS, :], value[:, ROWS:, :]
        return jnp.concatenate([left.reshape(LINE, hw), right.reshape(LINE, hw)], axis=1)

    eighth = lax.broadcasted_iota(jnp.int32, (LANES, 4 * LANES), 0) // 8
    block = lax.broadcasted_iota(jnp.int32, (LANES, 4 * LANES), 1) // LANES
    pick = ((eighth == block + jnp.where(block < 2, 3, 6)) | (eighth == block + 10)).astype(F32).astype(BF16)
    lane = lax.broadcasted_iota(jnp.int32, (8, LANES), 1)
    own_state = lane % 8 == lax.broadcasted_iota(jnp.int32, (8, LANES), 0)

    def prepare(cells, first):
        weight = w_xt[40 * first : 40 * first + 80, :]
        proj = lax.dot_general(cells, weight, (((1,), (1,)), ((), ())), preferred_element_type=F32)
        cells_float = cells.astype(F32)
        ranks = w_dt[...].astype(F32)
        for side in range(2):
            k = first + side
            low = proj[:, 40 * side : 40 * side + 24].astype(BF16)
            rank = ranks[24 * k : 24 * k + 24].astype(BF16)
            step = softplus(jnp.dot(low, rank, preferred_element_type=F32) + dt_bias[k : k + 1, :])
            push = step * cells_float
            for g in range(groups):
                steps[k, g, :LINE] = step[:, g * LANES : (g + 1) * LANES]
                drive[k, g, :LINE] = push[:, g * LANES : (g + 1) * LANES]
        proj = jnp.concatenate([proj, jnp.zeros((LINE, LANES - 80), F32)], axis=1)
        high = rounded(proj)
        left = rounded(proj - high)
        wide = lax.broadcasted_iota(jnp.int32, (LINE, LANES), 1)
        cell_maps[:LINE] = jnp.where(wide < 80, high, jnp.where(wide < 96, pltpu.roll(left, 56, 1), pltpu.roll(left, 32, 1)))
        rows = [jnp.where(own_state, cell_maps[pl.ds(cell, 8, stride=0), :], 0.0) for cell in range(LINE)]
        maps = jnp.dot(jnp.concatenate(rows, axis=0).astype(BF16), pick, preferred_element_type=F32)
        maps = maps.reshape(LINE, 8, 4 * LANES)
        for side in range(2):
            in_map[first + side] = maps[:, :, 2 * side * LANES : (2 * side + 1) * LANES]
            out_map[first + side] = maps[:, :, (2 * side + 1) * LANES : (2 * side + 2) * LANES]

    sub = lax.broadcasted_iota(jnp.int32, (8, LANES), 0)

    def scan(k, backward, start, total, first, finish=None):
        rates = -jnp.exp(a_log[k]) * LOG2E
        masks = [lax.rem(sub // s, 2) == backward for s in (1, 2, 4)]

        def chunk(turn, state):
            base = pl.multiple_of((turn + backward * (LINE // 8 - 1 - 2 * turn)) * 8, 8)
            cell = [base + i + backward * (7 - 2 * i) for i in range(8)]
            state = list(state)
            for g in range(groups):
                lanes = slice(g * LANES, (g + 1) * LANES)
                parts = []
                for i in range(8):
                    step = steps[k, g, pl.ds(cell[i], 8, stride=0), :]
                    push = drive[k, g, pl.ds(cell[i], 8, stride=0), :]
                    state[g] = jnp.exp2(step * rates[:, lanes]) * state[g] + in_map[k, cell[i]] * push
                    parts.append(out_map[k, cell[i]] * state[g])
                for s, mask in zip((1, 2, 4), masks):
                    parts = [
                        jnp.where(mask, a, b) + pltpu.roll(jnp.where(mask, b, a), s, 0)
                        for a, b in zip(parts[0::2], parts[1::2])
                    ]
                here = (pl.ds(base, 8), lanes)
                total[here] = parts[0] if first else total[here] + parts[0]
            return tuple(state)

        def pair(turn, state):
            state = chunk(2 * turn + 1, chunk(2 * turn, state))
            if finish is not None:
                finish(turn + backward * (LINE // 16 - 1 - 2 * turn))
            return state

        return lax.fori_loop(0, LINE // 16, pair, start)

    def split(state):
        return tuple(state[:, g * LANES : (g + 1) * LANES] for g in range(width // LANES))

    zero = tuple(jnp.zeros((8, LANES), F32) for _ in range(width // LANES))
    state_copies = [
        copy(state_out.at[0], state_in.at[0], state_send.at[0], state_recv.at[0], over_x),
        copy(state_out.at[1], state_in.at[1], state_send.at[1], state_recv.at[1], over_y),
    ]

    def wait_row(turn, carry):
        member = lax.rem(member_x + turn, ROWS)
        copy(row_out.at[member], row_in.at[member], row_send.at[member], row_recv.at[member], in_row(member)).wait_recv()
        return carry

    def wait_col(turn, carry):
        member = lax.rem(member_y + turn, COLS)
        copy(col_out.at[member], col_in.at[member], col_send.at[member], col_recv.at[member], in_col(member)).wait_recv()
        return carry

    def send_state(index, state):
        for g in range(width // LANES):
            state_out[index, :, g * LANES : (g + 1) * LANES] = state[g]
        state_copies[index].start()

    lax.fori_loop(1, ROWS, wait_row, 0)
    row_cells = row_in[...].reshape(LINE, width)
    prepare(row_cells, 0)
    send_state(0, scan(half_x, half_x, zero, row_sum, True))

    lax.fori_loop(own_col, COLS, wait_col, 0)
    col_cells = split_columns(col_in[...]).astype(BF16)
    prepare(col_cells, 2)
    send_state(1, scan(2 + half_y, half_y, zero, col_sum, True))

    def row_back(member, slot):
        return copy(row_back_out.at[member], row_back_in.at[slot], row_back_send.at[member], row_back_recv.at[slot], in_row(member))

    def col_back(member, slot):
        return copy(col_back_out.at[member], col_back_in.at[slot], col_back_send.at[member], col_back_recv.at[slot], in_col(member))

    def finish_row(member):
        row_back_out[member] = row_sum[pl.ds(pl.multiple_of(member * COLS, COLS), COLS), :].astype(BF16)

        @pl.when(member != member_x)
        def _():
            row_back(member, member_x).start()

    def finish_col(two):
        for member in (2 * two, 2 * two + 1):
            value = col_sum[pl.ds(pl.multiple_of(member * ROWS, ROWS), ROWS), :]
            col_back_out[member] = jnp.concatenate([value[:, :hw], value[:, hw:]], axis=0).astype(BF16)

            @pl.when((member != member_y) | (own_col == 0))
            def _():
                col_back(member, member_y).start()

    state_copies[1].wait_recv()
    scan(3 - half_y, 1 - half_y, split(state_in[1]), col_sum, False, finish_col)
    state_copies[0].wait_recv()
    scan(1 - half_x, 1 - half_x, split(state_in[0]), row_sum, False, finish_row)
    row_back_in[member_x] = row_back_out[member_x]

    @pl.when(own_col == 1)
    def _():
        col_back_in[member_y] = col_back_out[member_y]

    def wait_row_back(turn, carry):
        member = lax.rem(member_x + turn, ROWS)
        row_back(member, member).wait_recv()
        return carry

    def wait_col_back(turn, carry):
        member = lax.rem(member_y + turn, COLS)
        col_back(member, member).wait_recv()
        return carry

    lax.fori_loop(1, ROWS, wait_row_back, 0)
    row_value = row_back_in[...].reshape(LINE, width).astype(F32)
    for g in range(groups):
        summed[g, :LINE] = summed[g, :LINE] + row_value[:, g * LANES : (g + 1) * LANES]
    lax.fori_loop(own_col, COLS, wait_col_back, 0)
    for c in range(COLS):
        value = col_back_in[c].astype(F32)
        for g in range(groups):
            here = (g, pl.ds(c, ROWS, stride=COLS), slice(None))
            low, high = (0, ROWS) if g < groups // 2 else (ROWS, 2 * ROWS)
            lane = (g % (groups // 2)) * LANES
            summed[here] = summed[here] + value[low:high, lane : lane + LANES]
    total = jnp.concatenate([summed[g, :LINE] for g in range(groups)], axis=1)
    gated = (unit_norm(total) * out_gain[...].reshape(1, -1) + out_bias[...].reshape(1, -1)) * gate[...]
    mixed = tokens[...].astype(F32).reshape(ROWS * COLS, -1) + jnp.dot(gated.astype(BF16), w_out[...], preferred_element_type=F32)
    out[...] = mixed.reshape(out.shape).astype(BF16)

    for item in edges + state_copies:
        item.wait_send()

    def drain_row(turn, carry):
        member = lax.rem(member_x + turn, ROWS)
        row_copy(member).wait_send()
        row_back(member, member_x).wait_send()
        return carry

    def drain_col(turn, carry):
        member = lax.rem(member_y + turn, COLS)
        col_copy(member).wait_send()
        col_back(member, member_y).wait_send()
        return carry

    lax.fori_loop(1, ROWS, drain_row, 0)
    lax.fori_loop(own_col, COLS, drain_col, 0)


def shards(tokens, norm_gain, norm_bias, w_in, conv_taps, conv_bias, w_x, w_dt, dt_bias, a_log, d_skip, out_gain, out_bias, w_out):
    chans, width = tokens.shape[-1], w_out.shape[0]
    hw = width // 2
    dma = pltpu.SemaphoreType.DMA
    operands = (
        tokens, w_in, norm_gain, norm_bias, conv_taps, conv_bias, jnp.transpose(w_x, (0, 2, 1)).reshape(-1, width),
        w_dt.reshape(-1, width), dt_bias, a_log, d_skip, out_gain, out_bias, w_out,
    )
    return pl.pallas_call(
        kernel,
        out_shape=jax.ShapeDtypeStruct(tokens.shape, tokens.dtype),
        in_specs=[pl.BlockSpec(memory_space=pltpu.MemorySpace.HBM)] * 14,
        out_specs=pl.BlockSpec(memory_space=pltpu.VMEM),
        scratch_shapes=[pltpu.VMEM(value.shape, value.dtype) for value in operands] + [
            dma((14,)),
            pltpu.VMEM((6, ROWS, chans), F32),
            pltpu.VMEM((2, COLS, chans), BF16),
            pltpu.VMEM((2, ROWS, chans), F32),
            pltpu.VMEM((2, COLS, chans), BF16),
            pltpu.VMEM((ROWS + 2, COLS + 16, width), F32),
            pltpu.VMEM((4, COLS + 16, width), F32),
            pltpu.VMEM((width // LANES, LINE + COLS, LANES), F32),
            pltpu.VMEM((width // LANES, LINE + COLS, LANES), F32),
            pltpu.VMEM((ROWS * COLS, width), F32),
            pltpu.VMEM((ROWS, COLS, width), BF16),
            pltpu.VMEM((COLS, 2 * ROWS, hw), BF16),
            pltpu.VMEM((ROWS, COLS, width), BF16),
            pltpu.VMEM((COLS, 2 * ROWS, hw), BF16),
            pltpu.VMEM((LINE + 8, LANES), F32),
            pltpu.VMEM((4, width // LANES, LINE + 8, LANES), F32),
            pltpu.VMEM((4, width // LANES, LINE + 8, LANES), F32),
            pltpu.VMEM((4, LINE, 8, LANES), F32),
            pltpu.VMEM((4, LINE, 8, LANES), F32),
            pltpu.VMEM((LINE, width), F32),
            pltpu.VMEM((LINE, width), F32),
            pltpu.VMEM((2, 8, width), F32),
            pltpu.VMEM((2, 8, width), F32),
            pltpu.VMEM((ROWS, COLS, width), BF16),
            pltpu.VMEM((COLS, 2 * ROWS, hw), BF16),
            pltpu.VMEM((ROWS, COLS, width), BF16),
            pltpu.VMEM((COLS, 2 * ROWS, hw), BF16),
            dma((8,)), dma((8,)), dma((ROWS,)), dma((ROWS,)), dma((COLS,)), dma((COLS,)), dma((2,)), dma((2,)),
            dma((ROWS,)), dma((ROWS,)), dma((COLS,)), dma((COLS,)),
        ],
        compiler_params=pltpu.CompilerParams(collective_id=0, has_side_effects=True, vmem_limit_bytes=60 * 1024 * 1024),
    )(*operands)


def solution(mesh):
    placed = (P("gy", "gx", None),) + (P(),) * 13
    return jax.shard_map(shards, mesh=mesh, in_specs=placed, out_specs=P("gy", "gx", None), check_vma=False)
```

```python
import functools

import jax
import jax.numpy as jnp
from jax import lax
from jax.experimental import pallas as pl
from jax.experimental.pallas import tpu as pltpu
from jax.sharding import PartitionSpec as P

MESH = pl.DeviceIdType.MESH
F32 = jnp.float32
BF16 = jnp.bfloat16
LOG2E = 1.4426950408889634
ROWS, COLS = 8, 16
LINE = 128
LANES = 128


def rounded(value):
    return value.astype(BF16).astype(F32)


def unit_norm(values):
    mean = jnp.mean(values, axis=-1, keepdims=True)
    centred = values - mean
    spread = jnp.mean(centred * centred, axis=-1, keepdims=True)
    return centred * lax.rsqrt(spread + 1e-05)


def softplus(value):
    return jnp.maximum(value, 0.0) + jnp.log1p(jnp.exp(-jnp.abs(value)))


def silu(value):
    return value / (1.0 + jnp.exp(-value))


def kernel(
    tokens_hbm, w_in_hbm, norm_gain_hbm, norm_bias_hbm, taps_hbm, conv_bias_hbm, w_xt_hbm, w_dt_hbm, dt_bias_hbm, a_log_hbm,
    d_skip_hbm, out_gain_hbm, out_bias_hbm, w_out_hbm,
    out,
    tokens, w_in, norm_gain, norm_bias, taps, conv_bias, w_xt, w_dt, dt_bias, a_log, d_skip, out_gain, out_bias, w_out,
    load_sem,
    edge, edge_row, edge_col, halo, padded, beside, conved, summed, gate, row_out, col_out, row_in, col_in,
    cell_maps, spread, steps, drive, in_map, out_map, row_sum, col_sum, state_out, state_in,
    row_back_out, col_back_out, row_back_in, col_back_in,
    edge_send, edge_recv, row_send, row_recv, col_send, col_recv, state_send, state_recv,
    row_back_send, row_back_recv, col_back_send, col_back_recv,
):
    ny, nx = lax.axis_size("gy"), lax.axis_size("gx")
    my_y, my_x = lax.axis_index("gy"), lax.axis_index("gx")
    half_x, member_x = my_x // ROWS, lax.rem(my_x, ROWS)
    member_y = lax.rem(my_y, COLS)
    half_y = lax.rem(my_x, 2)
    own_col = (my_y // COLS == half_y).astype(jnp.int32)
    north, south = lax.rem(my_y + ny - 1, ny), lax.rem(my_y + 1, ny)
    west, east = lax.rem(my_x + nx - 1, nx), lax.rem(my_x + 1, nx)
    over_x = (my_y, lax.rem(my_x + ROWS, nx))
    over_y = (my_y, my_x + 1 - 2 * half_y)
    around = [(north, my_x), (south, my_x), (my_y, west), (my_y, east), (north, west), (north, east), (south, west), (south, east)]

    def in_row(member):
        return (my_y, half_x * ROWS + member)

    def in_col(member):
        return (half_y * COLS + member, my_x - half_y + my_y // COLS)

    pairs = [
        (tokens_hbm, tokens), (w_in_hbm, w_in), (norm_gain_hbm, norm_gain), (norm_bias_hbm, norm_bias), (taps_hbm, taps),
        (conv_bias_hbm, conv_bias), (w_xt_hbm, w_xt), (w_dt_hbm, w_dt), (dt_bias_hbm, dt_bias), (a_log_hbm, a_log),
        (d_skip_hbm, d_skip), (out_gain_hbm, out_gain), (out_bias_hbm, out_bias), (w_out_hbm, w_out),
    ]
    loads = [pltpu.make_async_copy(src, dst, load_sem.at[i]) for i, (src, dst) in enumerate(pairs)]
    loads[0].start()

    barrier = pltpu.get_barrier_semaphore()

    def greet(device):
        pl.semaphore_signal(barrier, inc=1, device_id=device, device_id_type=MESH)

    for device in around + [over_x, over_y]:
        greet(device)

    def greet_row(turn, carry):
        greet(in_row(lax.rem(member_x + turn, ROWS)))
        return carry

    def greet_col(turn, carry):
        greet(in_col(lax.rem(member_y + turn, COLS)))
        return carry

    lax.fori_loop(1, ROWS, greet_row, 0)
    lax.fori_loop(own_col, COLS, greet_col, 0)
    for item in loads[1:]:
        item.start()

    def copy(src, dst, send, recv, device):
        return pltpu.make_async_remote_copy(
            src_ref=src, dst_ref=dst, send_sem=send, recv_sem=recv, device_id=device, device_id_type=MESH
        )

    loads[0].wait()
    token_float = tokens[...].astype(F32)
    for r in range(ROWS):
        edge_col[0, r : r + 1, :] = token_float[r, 0:1, :]
        edge_col[1, r : r + 1, :] = token_float[r, COLS - 1 : COLS, :]
    edge_row[0] = tokens[0]
    edge_row[1] = tokens[ROWS - 1]
    pl.semaphore_wait(barrier, 10 + ROWS - 1 + COLS - own_col)
    sends = [
        (edge_row.at[0], halo.at[1], 1, around[0]),
        (edge_row.at[1], halo.at[0], 0, around[1]),
        (edge_col.at[0], edge.at[1], 3, around[2]),
        (edge_col.at[1], edge.at[0], 2, around[3]),
        (edge_col.at[0, pl.ds(0, 1)], edge.at[5, pl.ds(0, 1)], 7, around[4]),
        (edge_col.at[1, pl.ds(0, 1)], edge.at[4, pl.ds(0, 1)], 6, around[5]),
        (edge_col.at[0, pl.ds(7, 1)], edge.at[3, pl.ds(7, 1)], 5, around[6]),
        (edge_col.at[1, pl.ds(7, 1)], edge.at[2, pl.ds(7, 1)], 4, around[7]),
    ]
    edges = [copy(src, dst, edge_send.at[slot], edge_recv.at[slot], device) for src, dst, slot, device in sends]
    for item in edges:
        item.start()

    for item in loads[1:]:
        item.wait()
    gain, bias = norm_gain[...].reshape(1, -1), norm_bias[...].reshape(1, -1)

    def project(cells, weight):
        normed = (unit_norm(cells) * gain + bias).astype(BF16)
        return rounded(jnp.dot(normed, weight, preferred_element_type=F32))

    cells = token_float.reshape(ROWS * COLS, -1)
    normed = (unit_norm(cells) * gain + bias).astype(BF16)
    width = gate.shape[1]
    hw, groups = width // 2, width // LANES
    inner = rounded(jnp.dot(normed, w_in[:, :width], preferred_element_type=F32))
    padded[...] = jnp.zeros(padded.shape, F32)
    padded[1 : 1 + ROWS, 8 : 8 + COLS, :] = inner.reshape(ROWS, COLS, width)
    gate[...] = silu(rounded(jnp.dot(normed, w_in[:, width:], preferred_element_type=F32)))

    def conv_row(r, carry):
        total = jnp.broadcast_to(conv_bias[...].reshape(1, -1), (COLS, width))
        for i in range(3):
            for j in range(3):
                tap = 3 * i + j
                total = total + padded[r + i, 7 + j : 7 + j + COLS, :] * taps[tap : tap + 1, :]
        for g in range(groups):
            conved[g, pl.ds(pl.multiple_of(r * COLS, COLS), COLS), :] = total[:, g * LANES : (g + 1) * LANES]
        return carry

    lax.fori_loop(0, ROWS, conv_row, 0)
    for item in edges:
        item.wait_recv()
    rim = jnp.concatenate(
        [
            halo[0].astype(F32), halo[1].astype(F32), edge[0], edge[1],
            edge[2, 7:8, :], edge[3, 7:8, :], edge[4, 0:1, :], edge[5, 0:1, :], edge[0, 0:4, :],
        ],
        axis=0,
    )
    rim = project(rim, w_in[:, :width])
    has_n = (my_y > 0).astype(F32)
    has_s = (my_y < ny - 1).astype(F32)
    has_w = (my_x > 0).astype(F32)
    has_e = (my_x < nx - 1).astype(F32)
    beside[0, 8 : 8 + COLS, :] = rim[0:16] * has_n
    beside[0, 7:8, :] = rim[48:49] * (has_n * has_w)
    beside[0, 8 + COLS : 9 + COLS, :] = rim[49:50] * (has_n * has_e)
    beside[1, 8 : 8 + COLS, :] = rim[16:32] * has_s
    beside[1, 7:8, :] = rim[50:51] * (has_s * has_w)
    beside[1, 8 + COLS : 9 + COLS, :] = rim[51:52] * (has_s * has_e)
    nothing = jnp.zeros((8, width), F32)
    for side, value in ((2, rim[32:40] * has_w), (3, rim[40:48] * has_e)):
        beside[side, 0:8, :] = nothing
        beside[side, 8:16, :] = value
        beside[side, 16:24, :] = nothing
    for side, row in ((0, 0), (1, ROWS - 1)):
        more = sum(beside[side, 7 + j : 7 + j + COLS, :] * taps[6 * side + j : 6 * side + j + 1, :] for j in range(3))
        for g in range(groups):
            here = (g, slice(row * COLS, row * COLS + COLS))
            conved[here] = conved[here] + more[:, g * LANES : (g + 1) * LANES]
    for side, col in ((2, 0), (3, COLS - 1)):
        tap = 0 if side == 2 else 2
        more = sum(beside[side, 7 + i : 15 + i, :] * taps[3 * i + tap : 3 * i + tap + 1, :] for i in range(3))
        for g in range(groups):
            here = (g, pl.ds(col, ROWS, stride=COLS))
            conved[here] = conved[here] + more[:, g * LANES : (g + 1) * LANES]

    def settle_rows(src, dst, send, recv, what):
        item = copy(src.at[pl.ds(0, ROWS - 1)], dst.at[pl.ds(0, ROWS - 1)], send.at[0], recv.at[0], over_x)
        getattr(item, what)()

    def settle_cols(src, dst, send, recv, what):
        for own in range(2):

            @pl.when(own_col == own)
            def _(own=own):
                here = pl.ds(0, COLS - own)
                getattr(copy(src.at[here], dst.at[here], send.at[0], recv.at[0], over_y), what)()

    def row_copy(member):
        return copy(row_out.at[member], row_in.at[member_x], row_send.at[0], row_recv.at[0], in_row(member))

    def col_copy(member):
        return copy(col_out.at[member], col_in.at[member_y], col_send.at[0], col_recv.at[0], in_col(member))

    for r in range(ROWS):
        for g in range(groups):
            here = (g, slice(r * COLS, r * COLS + COLS))
            value = silu(conved[here]).astype(BF16)
            row_out[r, :, g * LANES : (g + 1) * LANES] = value
            conved[here] = value.astype(F32)
    for c in range(COLS):
        column = [conved[g, pl.ds(c, ROWS, stride=COLS), :] for g in range(groups)]
        for g in range(groups // 2):
            both = jnp.concatenate([column[g], column[g + groups // 2]], axis=0)
            col_out[c, :, g * LANES : (g + 1) * LANES] = both.astype(BF16)

    def start_col(turn, carry):
        col_copy(lax.rem(member_y + turn, COLS)).start()
        return carry

    def start_row(turn, carry):
        row_copy(lax.rem(member_x + turn, ROWS)).start()
        return carry

    lax.fori_loop(own_col, COLS, start_col, 0)
    lax.fori_loop(1, ROWS, start_row, 0)
    row_in[member_x] = row_out[member_x]

    @pl.when(own_col == 1)
    def _():
        col_in[member_y] = col_out[member_y]

    skip = jnp.sum(d_skip[...], axis=0, keepdims=True)
    for g in range(groups):
        summed[g, :LINE] = skip[:, g * LANES : (g + 1) * LANES] * conved[g, :LINE]

    def split_columns(stacked):
        value = stacked.astype(F32)
        left, right = value[:, :ROWS, :], value[:, ROWS:, :]
        return jnp.concatenate([left.reshape(LINE, hw), right.reshape(LINE, hw)], axis=1)

    eighth = lax.broadcasted_iota(jnp.int32, (LANES, 4 * LANES), 0) // 8
    block = lax.broadcasted_iota(jnp.int32, (LANES, 4 * LANES), 1) // LANES
    pick = ((eighth == block + jnp.where(block < 2, 3, 6)) | (eighth == block + 10)).astype(F32).astype(BF16)
    lane = lax.broadcasted_iota(jnp.int32, (8, LANES), 1)
    own_state = lane % 8 == lax.broadcasted_iota(jnp.int32, (8, LANES), 0)

    def project_maps(cells, line):
        weight = w_xt[80 * line : 80 * line + 80, :]
        proj = lax.dot_general(cells, weight, (((1,), (1,)), ((), ())), preferred_element_type=F32)
        proj = jnp.concatenate([proj, jnp.zeros((LINE, LANES - 80), F32)], axis=1)
        high = rounded(proj)
        left = rounded(proj - high)
        wide = lax.broadcasted_iota(jnp.int32, (LINE, LANES), 1)
        cell_maps[line, :LINE] = jnp.where(wide < 80, high, jnp.where(wide < 96, pltpu.roll(left, 56, 1), pltpu.roll(left, 32, 1)))
        rows = [jnp.where(own_state, cell_maps[line, pl.ds(cell, 8, stride=0), :], 0.0) for cell in range(LINE)]
        spread[line] = jnp.concatenate(rows, axis=0).astype(BF16)

    def prepare(cells, line, side):
        k = 2 * line + side
        first = side == 0
        low = cell_maps[line, :LINE]
        low = jnp.where(first, low[:, 0:24], low[:, 40:64]).astype(BF16)
        ranks = w_dt[48 * line : 48 * line + 48, :].astype(F32)
        rank = jnp.where(first, ranks[0:24], ranks[24:48]).astype(BF16)
        offset = jnp.where(first, dt_bias[2 * line : 2 * line + 1, :], dt_bias[2 * line + 1 : 2 * line + 2, :])
        step = softplus(jnp.dot(low, rank, preferred_element_type=F32) + offset)
        push = step * cells.astype(F32)
        for g in range(groups):
            steps[k, g, :LINE] = step[:, g * LANES : (g + 1) * LANES]
            drive[k, g, :LINE] = push[:, g * LANES : (g + 1) * LANES]
        wanted = jnp.where(first, pick[:, : 2 * LANES], pick[:, 2 * LANES :])
        maps = jnp.dot(spread[line], wanted, preferred_element_type=F32).reshape(LINE, 8, 2 * LANES)
        in_map[k] = maps[:, :, :LANES]
        out_map[k] = maps[:, :, LANES:]

    sub = lax.broadcasted_iota(jnp.int32, (8, LANES), 0)

    def scan(k, backward, start, total, first, finish=None):
        rates = -jnp.exp(a_log[k]) * LOG2E
        masks = [lax.rem(sub // s, 2) == backward for s in (1, 2, 4)]

        def chunk(turn, state):
            base = pl.multiple_of((turn + backward * (LINE // 8 - 1 - 2 * turn)) * 8, 8)
            cell = [base + i + backward * (7 - 2 * i) for i in range(8)]
            state = list(state)
            for g in range(groups):
                lanes = slice(g * LANES, (g + 1) * LANES)
                parts = []
                for i in range(8):
                    step = steps[k, g, pl.ds(cell[i], 8, stride=0), :]
                    push = drive[k, g, pl.ds(cell[i], 8, stride=0), :]
                    state[g] = jnp.exp2(step * rates[:, lanes]) * state[g] + in_map[k, cell[i]] * push
                    parts.append(out_map[k, cell[i]] * state[g])
                for s, mask in zip((1, 2, 4), masks):
                    parts = [
                        jnp.where(mask, a, b) + pltpu.roll(jnp.where(mask, b, a), s, 0)
                        for a, b in zip(parts[0::2], parts[1::2])
                    ]
                here = (pl.ds(base, 8), lanes)
                total[here] = parts[0] if first else total[here] + parts[0]
            return tuple(state)

        def pair(turn, state):
            state = chunk(2 * turn + 1, chunk(2 * turn, state))
            if finish is not None:
                finish(turn + backward * (LINE // 16 - 1 - 2 * turn))
            return state

        return lax.fori_loop(0, LINE // 16, pair, start)

    def split(state):
        return tuple(state[:, g * LANES : (g + 1) * LANES] for g in range(width // LANES))

    zero = tuple(jnp.zeros((8, LANES), F32) for _ in range(width // LANES))
    state_copies = [
        copy(state_out.at[0], state_in.at[0], state_send.at[0], state_recv.at[0], over_x),
        copy(state_out.at[1], state_in.at[1], state_send.at[1], state_recv.at[1], over_y),
    ]

    def send_state(index, state):
        for g in range(width // LANES):
            state_out[index, :, g * LANES : (g + 1) * LANES] = state[g]
        state_copies[index].start()

    settle_rows(row_out, row_in, row_send, row_recv, "wait_recv")
    row_cells = row_in[...].reshape(LINE, width)
    project_maps(row_cells, 0)
    prepare(row_cells, 0, half_x)
    send_state(0, scan(half_x, half_x, zero, row_sum, True))

    settle_cols(col_out, col_in, col_send, col_recv, "wait_recv")
    col_cells = split_columns(col_in[...]).astype(BF16)
    project_maps(col_cells, 1)
    prepare(col_cells, 1, half_y)
    send_state(1, scan(2 + half_y, half_y, zero, col_sum, True))

    def row_back(member, slot):
        return copy(row_back_out.at[member], row_back_in.at[slot], row_back_send.at[0], row_back_recv.at[0], in_row(member))

    def col_back(member, slot):
        return copy(col_back_out.at[member], col_back_in.at[slot], col_back_send.at[0], col_back_recv.at[0], in_col(member))

    def finish_row(member):
        row_back_out[member] = row_sum[pl.ds(pl.multiple_of(member * COLS, COLS), COLS), :].astype(BF16)

        @pl.when(member != member_x)
        def _():
            row_back(member, member_x).start()

    def finish_col(two):
        for member in (2 * two, 2 * two + 1):
            value = col_sum[pl.ds(pl.multiple_of(member * ROWS, ROWS), ROWS), :]
            col_back_out[member] = jnp.concatenate([value[:, :hw], value[:, hw:]], axis=0).astype(BF16)

            @pl.when((member != member_y) | (own_col == 0))
            def _():
                col_back(member, member_y).start()

    prepare(col_cells, 1, 1 - half_y)
    state_copies[1].wait_recv()
    scan(3 - half_y, 1 - half_y, split(state_in[1]), col_sum, False, finish_col)
    prepare(row_in[...].reshape(LINE, width), 0, 1 - half_x)
    state_copies[0].wait_recv()
    scan(1 - half_x, 1 - half_x, split(state_in[0]), row_sum, False, finish_row)
    row_back_in[member_x] = row_back_out[member_x]

    @pl.when(own_col == 1)
    def _():
        col_back_in[member_y] = col_back_out[member_y]

    for item in edges + state_copies:
        item.wait_send()
    settle_rows(row_out, row_in, row_send, row_recv, "wait_send")
    settle_cols(col_out, col_in, col_send, col_recv, "wait_send")
    settle_rows(row_back_out, row_back_in, row_back_send, row_back_recv, "wait_recv")
    row_value = row_back_in[...].reshape(LINE, width).astype(F32)
    for g in range(groups):
        summed[g, :LINE] = summed[g, :LINE] + row_value[:, g * LANES : (g + 1) * LANES]
    settle_cols(col_back_out, col_back_in, col_back_send, col_back_recv, "wait_send")
    settle_rows(row_back_out, row_back_in, row_back_send, row_back_recv, "wait_send")
    settle_cols(col_back_out, col_back_in, col_back_send, col_back_recv, "wait_recv")
    for c in range(COLS):
        value = col_back_in[c].astype(F32)
        for g in range(groups):
            here = (g, pl.ds(c, ROWS, stride=COLS), slice(None))
            low, high = (0, ROWS) if g < groups // 2 else (ROWS, 2 * ROWS)
            lane = (g % (groups // 2)) * LANES
            summed[here] = summed[here] + value[low:high, lane : lane + LANES]
    total = jnp.concatenate([summed[g, :LINE] for g in range(groups)], axis=1)
    gated = (unit_norm(total) * out_gain[...].reshape(1, -1) + out_bias[...].reshape(1, -1)) * gate[...]
    mixed = tokens[...].astype(F32).reshape(ROWS * COLS, -1) + jnp.dot(gated.astype(BF16), w_out[...], preferred_element_type=F32)
    out[...] = mixed.reshape(out.shape).astype(BF16)


def shards(tokens, norm_gain, norm_bias, w_in, conv_taps, conv_bias, w_x, w_dt, dt_bias, a_log, d_skip, out_gain, out_bias, w_out):
    chans, width = tokens.shape[-1], w_out.shape[0]
    hw = width // 2
    dma = pltpu.SemaphoreType.DMA
    operands = (
        tokens, w_in, norm_gain, norm_bias, conv_taps, conv_bias, jnp.transpose(w_x, (0, 2, 1)).reshape(-1, width),
        w_dt.reshape(-1, width), dt_bias, a_log, d_skip, out_gain, out_bias, w_out,
    )
    return pl.pallas_call(
        kernel,
        out_shape=jax.ShapeDtypeStruct(tokens.shape, tokens.dtype),
        in_specs=[pl.BlockSpec(memory_space=pltpu.MemorySpace.HBM)] * 14,
        out_specs=pl.BlockSpec(memory_space=pltpu.VMEM),
        scratch_shapes=[pltpu.VMEM(value.shape, value.dtype) for value in operands] + [
            dma((14,)),
            pltpu.VMEM((6, ROWS, chans), F32),
            pltpu.VMEM((2, COLS, chans), BF16),
            pltpu.VMEM((2, ROWS, chans), F32),
            pltpu.VMEM((2, COLS, chans), BF16),
            pltpu.VMEM((ROWS + 2, COLS + 16, width), F32),
            pltpu.VMEM((4, COLS + 16, width), F32),
            pltpu.VMEM((width // LANES, LINE + COLS, LANES), F32),
            pltpu.VMEM((width // LANES, LINE + COLS, LANES), F32),
            pltpu.VMEM((ROWS * COLS, width), F32),
            pltpu.VMEM((ROWS, COLS, width), BF16),
            pltpu.VMEM((COLS, 2 * ROWS, hw), BF16),
            pltpu.VMEM((ROWS, COLS, width), BF16),
            pltpu.VMEM((COLS, 2 * ROWS, hw), BF16),
            pltpu.VMEM((2, LINE + 8, LANES), F32),
            pltpu.VMEM((2, LINE * 8, LANES), BF16),
            pltpu.VMEM((4, width // LANES, LINE + 8, LANES), F32),
            pltpu.VMEM((4, width // LANES, LINE + 8, LANES), F32),
            pltpu.VMEM((4, LINE, 8, LANES), F32),
            pltpu.VMEM((4, LINE, 8, LANES), F32),
            pltpu.VMEM((LINE, width), F32),
            pltpu.VMEM((LINE, width), F32),
            pltpu.VMEM((2, 8, width), F32),
            pltpu.VMEM((2, 8, width), F32),
            pltpu.VMEM((ROWS, COLS, width), BF16),
            pltpu.VMEM((COLS, 2 * ROWS, hw), BF16),
            pltpu.VMEM((ROWS, COLS, width), BF16),
            pltpu.VMEM((COLS, 2 * ROWS, hw), BF16),
            dma((8,)), dma((8,)), dma((1,)), dma((1,)), dma((1,)), dma((1,)), dma((2,)), dma((2,)),
            dma((1,)), dma((1,)), dma((1,)), dma((1,)),
        ],
        compiler_params=pltpu.CompilerParams(collective_id=0, has_side_effects=True, vmem_limit_bytes=60 * 1024 * 1024),
    )(*operands)


def solution(mesh):
    placed = (P("gy", "gx", None),) + (P(),) * 13
    return jax.shard_map(shards, mesh=mesh, in_specs=placed, out_specs=P("gy", "gx", None), check_vma=False)
```

```python
import functools

import jax
import jax.numpy as jnp
from jax import lax
from jax.experimental import pallas as pl
from jax.experimental.pallas import tpu as pltpu
from jax.sharding import PartitionSpec as P

MESH = pl.DeviceIdType.MESH
F32 = jnp.float32
BF16 = jnp.bfloat16
LOG2E = 1.4426950408889634
ROWS, COLS = 8, 16
LINE = 128
LANES = 128


def rounded(value):
    return value.astype(BF16).astype(F32)


def unit_norm(values):
    mean = jnp.mean(values, axis=-1, keepdims=True)
    centred = values - mean
    spread = jnp.mean(centred * centred, axis=-1, keepdims=True)
    return centred * lax.rsqrt(spread + 1e-05)


def softplus(value):
    return jnp.maximum(value, 0.0) + jnp.log1p(jnp.exp(-jnp.abs(value)))


def silu(value):
    return value / (1.0 + jnp.exp(-value))


def kernel(
    tokens_hbm, w_in_hbm, norm_gain_hbm, norm_bias_hbm, taps_hbm, conv_bias_hbm, w_xt_hbm, w_dt_hbm, dt_bias_hbm, a_log_hbm,
    d_skip_hbm, out_gain_hbm, out_bias_hbm, w_out_hbm,
    out,
    tokens, w_in, norm_gain, norm_bias, taps, conv_bias, w_xt, w_dt, dt_bias, a_log, d_skip, out_gain, out_bias, w_out,
    load_sem,
    edge, edge_row, edge_col, halo, padded, beside, conved, summed, gate, row_out, col_out, row_in, col_in,
    cell_maps, spread, steps, drive, in_map, out_map, row_sum, col_sum, state_out, state_in,
    row_back_out, col_back_out, row_back_in, col_back_in,
    edge_send, edge_recv, row_send, row_recv, col_send, col_recv, state_send, state_recv,
    row_back_send, row_back_recv, col_back_send, col_back_recv,
):
    ny, nx = lax.axis_size("gy"), lax.axis_size("gx")
    my_y, my_x = lax.axis_index("gy"), lax.axis_index("gx")
    half_x, member_x = my_x // ROWS, lax.rem(my_x, ROWS)
    member_y = lax.rem(my_y, COLS)
    half_y = lax.rem(my_x, 2)
    own_col = (my_y // COLS == half_y).astype(jnp.int32)
    north, south = lax.rem(my_y + ny - 1, ny), lax.rem(my_y + 1, ny)
    west, east = lax.rem(my_x + nx - 1, nx), lax.rem(my_x + 1, nx)
    over_x = (my_y, lax.rem(my_x + ROWS, nx))
    over_y = (my_y, my_x + 1 - 2 * half_y)
    around = [(north, my_x), (south, my_x), (my_y, west), (my_y, east), (north, west), (north, east), (south, west), (south, east)]

    def in_row(member):
        return (my_y, half_x * ROWS + member)

    def in_col(member):
        return (half_y * COLS + member, my_x - half_y + my_y // COLS)

    pairs = [
        (tokens_hbm, tokens), (w_in_hbm, w_in), (norm_gain_hbm, norm_gain), (norm_bias_hbm, norm_bias), (taps_hbm, taps),
        (conv_bias_hbm, conv_bias), (w_xt_hbm, w_xt), (w_dt_hbm, w_dt), (dt_bias_hbm, dt_bias), (a_log_hbm, a_log),
        (d_skip_hbm, d_skip), (out_gain_hbm, out_gain), (out_bias_hbm, out_bias), (w_out_hbm, w_out),
    ]
    loads = [pltpu.make_async_copy(src, dst, load_sem.at[i]) for i, (src, dst) in enumerate(pairs)]
    loads[0].start()

    barrier = pltpu.get_barrier_semaphore()

    def greet(device):
        pl.semaphore_signal(barrier, inc=1, device_id=device, device_id_type=MESH)

    for device in around + [over_x, over_y]:
        greet(device)

    def greet_row(turn, carry):
        greet(in_row(lax.rem(member_x + turn, ROWS)))
        return carry

    def greet_col(turn, carry):
        greet(in_col(lax.rem(member_y + turn, COLS)))
        return carry

    for turn in range(1, COLS):
        greet_col(turn, 0)

    @pl.when(own_col == 0)
    def _():
        greet_col(0, 0)

    for turn in range(1, ROWS):
        greet_row(turn, 0)
    for item in loads[1:]:
        item.start()

    def copy(src, dst, send, recv, device):
        return pltpu.make_async_remote_copy(
            src_ref=src, dst_ref=dst, send_sem=send, recv_sem=recv, device_id=device, device_id_type=MESH
        )

    loads[0].wait()
    token_float = tokens[...].astype(F32)
    for r in range(ROWS):
        edge_col[0, r : r + 1, :] = token_float[r, 0:1, :]
        edge_col[1, r : r + 1, :] = token_float[r, COLS - 1 : COLS, :]
    edge_row[0] = tokens[0]
    edge_row[1] = tokens[ROWS - 1]
    pl.semaphore_wait(barrier, 10 + ROWS - 1 + COLS - own_col)
    sends = [
        (edge_row.at[0], halo.at[1], 1, around[0]),
        (edge_row.at[1], halo.at[0], 0, around[1]),
        (edge_col.at[0], edge.at[1], 3, around[2]),
        (edge_col.at[1], edge.at[0], 2, around[3]),
        (edge_col.at[0, pl.ds(0, 1)], edge.at[5, pl.ds(0, 1)], 7, around[4]),
        (edge_col.at[1, pl.ds(0, 1)], edge.at[4, pl.ds(0, 1)], 6, around[5]),
        (edge_col.at[0, pl.ds(7, 1)], edge.at[3, pl.ds(7, 1)], 5, around[6]),
        (edge_col.at[1, pl.ds(7, 1)], edge.at[2, pl.ds(7, 1)], 4, around[7]),
    ]
    edges = [copy(src, dst, edge_send.at[slot], edge_recv.at[slot], device) for src, dst, slot, device in sends]
    for item in edges:
        item.start()

    for item in loads[1:]:
        item.wait()
    gain, bias = norm_gain[...].reshape(1, -1), norm_bias[...].reshape(1, -1)

    def project(cells, weight):
        normed = (unit_norm(cells) * gain + bias).astype(BF16)
        return rounded(jnp.dot(normed, weight, preferred_element_type=F32))

    cells = token_float.reshape(ROWS * COLS, -1)
    normed = (unit_norm(cells) * gain + bias).astype(BF16)
    width = gate.shape[1]
    hw, groups = width // 2, width // LANES
    inner = rounded(jnp.dot(normed, w_in[:, :width], preferred_element_type=F32))
    padded[...] = jnp.zeros(padded.shape, F32)
    padded[1 : 1 + ROWS, 8 : 8 + COLS, :] = inner.reshape(ROWS, COLS, width)
    gate[...] = silu(rounded(jnp.dot(normed, w_in[:, width:], preferred_element_type=F32)))

    def conv_row(r, carry):
        total = jnp.broadcast_to(conv_bias[...].reshape(1, -1), (COLS, width))
        for i in range(3):
            for j in range(3):
                tap = 3 * i + j
                total = total + padded[r + i, 7 + j : 7 + j + COLS, :] * taps[tap : tap + 1, :]
        for g in range(groups):
            conved[g, pl.ds(pl.multiple_of(r * COLS, COLS), COLS), :] = total[:, g * LANES : (g + 1) * LANES]
        return carry

    lax.fori_loop(0, ROWS, conv_row, 0)
    for item in edges:
        item.wait_recv()
    rim = jnp.concatenate(
        [
            halo[0].astype(F32), halo[1].astype(F32), edge[0], edge[1],
            edge[2, 7:8, :], edge[3, 7:8, :], edge[4, 0:1, :], edge[5, 0:1, :], edge[0, 0:4, :],
        ],
        axis=0,
    )
    rim = project(rim, w_in[:, :width])
    has_n = (my_y > 0).astype(F32)
    has_s = (my_y < ny - 1).astype(F32)
    has_w = (my_x > 0).astype(F32)
    has_e = (my_x < nx - 1).astype(F32)
    beside[0, 8 : 8 + COLS, :] = rim[0:16] * has_n
    beside[0, 7:8, :] = rim[48:49] * (has_n * has_w)
    beside[0, 8 + COLS : 9 + COLS, :] = rim[49:50] * (has_n * has_e)
    beside[1, 8 : 8 + COLS, :] = rim[16:32] * has_s
    beside[1, 7:8, :] = rim[50:51] * (has_s * has_w)
    beside[1, 8 + COLS : 9 + COLS, :] = rim[51:52] * (has_s * has_e)
    nothing = jnp.zeros((8, width), F32)
    for side, value in ((2, rim[32:40] * has_w), (3, rim[40:48] * has_e)):
        beside[side, 0:8, :] = nothing
        beside[side, 8:16, :] = value
        beside[side, 16:24, :] = nothing
    for side, row in ((0, 0), (1, ROWS - 1)):
        more = sum(beside[side, 7 + j : 7 + j + COLS, :] * taps[6 * side + j : 6 * side + j + 1, :] for j in range(3))
        for g in range(groups):
            here = (g, slice(row * COLS, row * COLS + COLS))
            conved[here] = conved[here] + more[:, g * LANES : (g + 1) * LANES]
    for side, col in ((2, 0), (3, COLS - 1)):
        tap = 0 if side == 2 else 2
        more = sum(beside[side, 7 + i : 15 + i, :] * taps[3 * i + tap : 3 * i + tap + 1, :] for i in range(3))
        for g in range(groups):
            here = (g, pl.ds(col, ROWS, stride=COLS))
            conved[here] = conved[here] + more[:, g * LANES : (g + 1) * LANES]

    def settle_rows(src, dst, send, recv, what):
        item = copy(src.at[pl.ds(0, ROWS - 1)], dst.at[pl.ds(0, ROWS - 1)], send.at[0], recv.at[0], over_x)
        getattr(item, what)()

    def settle_cols(src, dst, send, recv, what):
        for own in range(2):

            @pl.when(own_col == own)
            def _(own=own):
                here = pl.ds(0, COLS - own)
                getattr(copy(src.at[here], dst.at[here], send.at[0], recv.at[0], over_y), what)()

    def row_copy(member):
        return copy(row_out.at[member], row_in.at[member_x], row_send.at[0], row_recv.at[0], in_row(member))

    def col_copy(member):
        return copy(col_out.at[member], col_in.at[member_y], col_send.at[0], col_recv.at[0], in_col(member))

    for r in range(ROWS):
        for g in range(groups):
            here = (g, slice(r * COLS, r * COLS + COLS))
            value = silu(conved[here]).astype(BF16)
            row_out[r, :, g * LANES : (g + 1) * LANES] = value
            conved[here] = value.astype(F32)
    for c in range(COLS):
        column = [conved[g, pl.ds(c, ROWS, stride=COLS), :] for g in range(groups)]
        for g in range(groups // 2):
            both = jnp.concatenate([column[g], column[g + groups // 2]], axis=0)
            col_out[c, :, g * LANES : (g + 1) * LANES] = both.astype(BF16)

    def start_col(turn, carry):
        col_copy(lax.rem(member_y + turn, COLS)).start()
        return carry

    def start_row(turn, carry):
        row_copy(lax.rem(member_x + turn, ROWS)).start()
        return carry

    for turn in range(1, COLS):
        start_col(turn, 0)

    @pl.when(own_col == 0)
    def _():
        start_col(0, 0)

    for turn in range(1, ROWS):
        start_row(turn, 0)
    row_in[member_x] = row_out[member_x]

    @pl.when(own_col == 1)
    def _():
        col_in[member_y] = col_out[member_y]

    skip = jnp.sum(d_skip[...], axis=0, keepdims=True)
    for g in range(groups):
        summed[g, :LINE] = skip[:, g * LANES : (g + 1) * LANES] * conved[g, :LINE]

    def split_columns(stacked):
        value = stacked.astype(F32)
        left, right = value[:, :ROWS, :], value[:, ROWS:, :]
        return jnp.concatenate([left.reshape(LINE, hw), right.reshape(LINE, hw)], axis=1)

    eighth = lax.broadcasted_iota(jnp.int32, (LANES, 4 * LANES), 0) // 8
    block = lax.broadcasted_iota(jnp.int32, (LANES, 4 * LANES), 1) // LANES
    pick = ((eighth == block + jnp.where(block < 2, 3, 6)) | (eighth == block + 10)).astype(F32).astype(BF16)
    lane = lax.broadcasted_iota(jnp.int32, (8, LANES), 1)
    own_state = lane % 8 == lax.broadcasted_iota(jnp.int32, (8, LANES), 0)

    def project_maps(cells, line):
        weight = w_xt[80 * line : 80 * line + 80, :]
        proj = lax.dot_general(cells, weight, (((1,), (1,)), ((), ())), preferred_element_type=F32)
        proj = jnp.concatenate([proj, jnp.zeros((LINE, LANES - 80), F32)], axis=1)
        high = rounded(proj)
        left = rounded(proj - high)
        wide = lax.broadcasted_iota(jnp.int32, (LINE, LANES), 1)
        cell_maps[line, :LINE] = jnp.where(wide < 80, high, jnp.where(wide < 96, pltpu.roll(left, 56, 1), pltpu.roll(left, 32, 1)))
        rows = [jnp.where(own_state, cell_maps[line, pl.ds(cell, 8, stride=0), :], 0.0) for cell in range(LINE)]
        spread[line] = jnp.concatenate(rows, axis=0).astype(BF16)

    def prepare(cells, line, side):
        k = 2 * line + side
        first = side == 0
        low = cell_maps[line, :LINE]
        low = jnp.where(first, low[:, 0:24], low[:, 40:64]).astype(BF16)
        ranks = w_dt[48 * line : 48 * line + 48, :].astype(F32)
        rank = jnp.where(first, ranks[0:24], ranks[24:48]).astype(BF16)
        offset = jnp.where(first, dt_bias[2 * line : 2 * line + 1, :], dt_bias[2 * line + 1 : 2 * line + 2, :])
        step = softplus(jnp.dot(low, rank, preferred_element_type=F32) + offset)
        push = step * cells.astype(F32)
        for g in range(groups):
            steps[k, g, :LINE] = step[:, g * LANES : (g + 1) * LANES]
            drive[k, g, :LINE] = push[:, g * LANES : (g + 1) * LANES]
        wanted = jnp.where(first, pick[:, : 2 * LANES], pick[:, 2 * LANES :])
        maps = jnp.dot(spread[line], wanted, preferred_element_type=F32).reshape(LINE, 8, 2 * LANES)
        in_map[k] = maps[:, :, :LANES]
        out_map[k] = maps[:, :, LANES:]

    sub = lax.broadcasted_iota(jnp.int32, (8, LANES), 0)

    def scan(k, backward, start, total, first, finish=None):
        rates = -jnp.exp(a_log[k]) * LOG2E
        masks = [lax.rem(sub // s, 2) == backward for s in (1, 2, 4)]

        def chunk(turn, state):
            base = pl.multiple_of((turn + backward * (LINE // 8 - 1 - 2 * turn)) * 8, 8)
            cell = [base + i + backward * (7 - 2 * i) for i in range(8)]
            state = list(state)
            for g in range(groups):
                lanes = slice(g * LANES, (g + 1) * LANES)
                parts = []
                for i in range(8):
                    step = steps[k, g, pl.ds(cell[i], 8, stride=0), :]
                    push = drive[k, g, pl.ds(cell[i], 8, stride=0), :]
                    state[g] = jnp.exp2(step * rates[:, lanes]) * state[g] + in_map[k, cell[i]] * push
                    parts.append(out_map[k, cell[i]] * state[g])
                for s, mask in zip((1, 2, 4), masks):
                    parts = [
                        jnp.where(mask, a, b) + pltpu.roll(jnp.where(mask, b, a), s, 0)
                        for a, b in zip(parts[0::2], parts[1::2])
                    ]
                here = (pl.ds(base, 8), lanes)
                total[here] = parts[0] if first else total[here] + parts[0]
            return tuple(state)

        def pair(turn, state):
            state = chunk(2 * turn + 1, chunk(2 * turn, state))
            if finish is not None:
                finish(turn + backward * (LINE // 16 - 1 - 2 * turn))
            return state

        return lax.fori_loop(0, LINE // 16, pair, start)

    def split(state):
        return tuple(state[:, g * LANES : (g + 1) * LANES] for g in range(width // LANES))

    zero = tuple(jnp.zeros((8, LANES), F32) for _ in range(width // LANES))
    state_copies = [
        copy(state_out.at[0], state_in.at[0], state_send.at[0], state_recv.at[0], over_x),
        copy(state_out.at[1], state_in.at[1], state_send.at[1], state_recv.at[1], over_y),
    ]

    def send_state(index, state):
        for g in range(width // LANES):
            state_out[index, :, g * LANES : (g + 1) * LANES] = state[g]
        state_copies[index].start()

    settle_rows(row_out, row_in, row_send, row_recv, "wait_recv")
    row_cells = row_in[...].reshape(LINE, width)
    project_maps(row_cells, 0)
    prepare(row_cells, 0, half_x)
    send_state(0, scan(half_x, half_x, zero, row_sum, True))

    settle_cols(col_out, col_in, col_send, col_recv, "wait_recv")
    col_cells = split_columns(col_in[...]).astype(BF16)
    project_maps(col_cells, 1)
    prepare(col_cells, 1, half_y)
    send_state(1, scan(2 + half_y, half_y, zero, col_sum, True))

    def row_back(member, slot):
        return copy(row_back_out.at[member], row_back_in.at[slot], row_back_send.at[0], row_back_recv.at[0], in_row(member))

    def col_back(member, slot):
        return copy(col_back_out.at[member], col_back_in.at[slot], col_back_send.at[0], col_back_recv.at[0], in_col(member))

    def finish_row(member):
        row_back_out[member] = row_sum[pl.ds(pl.multiple_of(member * COLS, COLS), COLS), :].astype(BF16)

        @pl.when(member != member_x)
        def _():
            row_back(member, member_x).start()

    def finish_col(two):
        for member in (2 * two, 2 * two + 1):
            value = col_sum[pl.ds(pl.multiple_of(member * ROWS, ROWS), ROWS), :]
            col_back_out[member] = jnp.concatenate([value[:, :hw], value[:, hw:]], axis=0).astype(BF16)

            @pl.when((member != member_y) | (own_col == 0))
            def _():
                col_back(member, member_y).start()

    prepare(col_cells, 1, 1 - half_y)
    state_copies[1].wait_recv()
    scan(3 - half_y, 1 - half_y, split(state_in[1]), col_sum, False, finish_col)
    prepare(row_in[...].reshape(LINE, width), 0, 1 - half_x)
    state_copies[0].wait_recv()
    scan(1 - half_x, 1 - half_x, split(state_in[0]), row_sum, False, finish_row)
    row_back_in[member_x] = row_back_out[member_x]

    @pl.when(own_col == 1)
    def _():
        col_back_in[member_y] = col_back_out[member_y]

    for item in edges + state_copies:
        item.wait_send()
    settle_rows(row_out, row_in, row_send, row_recv, "wait_send")
    settle_cols(col_out, col_in, col_send, col_recv, "wait_send")
    settle_rows(row_back_out, row_back_in, row_back_send, row_back_recv, "wait_recv")
    row_value = row_back_in[...].reshape(LINE, width).astype(F32)
    for g in range(groups):
        summed[g, :LINE] = summed[g, :LINE] + row_value[:, g * LANES : (g + 1) * LANES]
    settle_cols(col_back_out, col_back_in, col_back_send, col_back_recv, "wait_send")
    settle_rows(row_back_out, row_back_in, row_back_send, row_back_recv, "wait_send")
    settle_cols(col_back_out, col_back_in, col_back_send, col_back_recv, "wait_recv")
    for c in range(COLS):
        value = col_back_in[c].astype(F32)
        for g in range(groups):
            here = (g, pl.ds(c, ROWS, stride=COLS), slice(None))
            low, high = (0, ROWS) if g < groups // 2 else (ROWS, 2 * ROWS)
            lane = (g % (groups // 2)) * LANES
            summed[here] = summed[here] + value[low:high, lane : lane + LANES]
    total = jnp.concatenate([summed[g, :LINE] for g in range(groups)], axis=1)
    gated = (unit_norm(total) * out_gain[...].reshape(1, -1) + out_bias[...].reshape(1, -1)) * gate[...]
    mixed = tokens[...].astype(F32).reshape(ROWS * COLS, -1) + jnp.dot(gated.astype(BF16), w_out[...], preferred_element_type=F32)
    out[...] = mixed.reshape(out.shape).astype(BF16)


def shards(tokens, norm_gain, norm_bias, w_in, conv_taps, conv_bias, w_x, w_dt, dt_bias, a_log, d_skip, out_gain, out_bias, w_out):
    chans, width = tokens.shape[-1], w_out.shape[0]
    hw = width // 2
    dma = pltpu.SemaphoreType.DMA
    operands = (
        tokens, w_in, norm_gain, norm_bias, conv_taps, conv_bias, jnp.transpose(w_x, (0, 2, 1)).reshape(-1, width),
        w_dt.reshape(-1, width), dt_bias, a_log, d_skip, out_gain, out_bias, w_out,
    )
    return pl.pallas_call(
        kernel,
        out_shape=jax.ShapeDtypeStruct(tokens.shape, tokens.dtype),
        in_specs=[pl.BlockSpec(memory_space=pltpu.MemorySpace.HBM)] * 14,
        out_specs=pl.BlockSpec(memory_space=pltpu.VMEM),
        scratch_shapes=[pltpu.VMEM(value.shape, value.dtype) for value in operands] + [
            dma((14,)),
            pltpu.VMEM((6, ROWS, chans), F32),
            pltpu.VMEM((2, COLS, chans), BF16),
            pltpu.VMEM((2, ROWS, chans), F32),
            pltpu.VMEM((2, COLS, chans), BF16),
            pltpu.VMEM((ROWS + 2, COLS + 16, width), F32),
            pltpu.VMEM((4, COLS + 16, width), F32),
            pltpu.VMEM((width // LANES, LINE + COLS, LANES), F32),
            pltpu.VMEM((width // LANES, LINE + COLS, LANES), F32),
            pltpu.VMEM((ROWS * COLS, width), F32),
            pltpu.VMEM((ROWS, COLS, width), BF16),
            pltpu.VMEM((COLS, 2 * ROWS, hw), BF16),
            pltpu.VMEM((ROWS, COLS, width), BF16),
            pltpu.VMEM((COLS, 2 * ROWS, hw), BF16),
            pltpu.VMEM((2, LINE + 8, LANES), F32),
            pltpu.VMEM((2, LINE * 8, LANES), BF16),
            pltpu.VMEM((4, width // LANES, LINE + 8, LANES), F32),
            pltpu.VMEM((4, width // LANES, LINE + 8, LANES), F32),
            pltpu.VMEM((4, LINE, 8, LANES), F32),
            pltpu.VMEM((4, LINE, 8, LANES), F32),
            pltpu.VMEM((LINE, width), F32),
            pltpu.VMEM((LINE, width), F32),
            pltpu.VMEM((2, 8, width), F32),
            pltpu.VMEM((2, 8, width), F32),
            pltpu.VMEM((ROWS, COLS, width), BF16),
            pltpu.VMEM((COLS, 2 * ROWS, hw), BF16),
            pltpu.VMEM((ROWS, COLS, width), BF16),
            pltpu.VMEM((COLS, 2 * ROWS, hw), BF16),
            dma((8,)), dma((8,)), dma((1,)), dma((1,)), dma((1,)), dma((1,)), dma((2,)), dma((2,)),
            dma((1,)), dma((1,)), dma((1,)), dma((1,)),
        ],
        compiler_params=pltpu.CompilerParams(collective_id=0, has_side_effects=True, vmem_limit_bytes=60 * 1024 * 1024),
    )(*operands)


def solution(mesh):
    placed = (P("gy", "gx", None),) + (P(),) * 13
    return jax.shard_map(shards, mesh=mesh, in_specs=placed, out_specs=P("gy", "gx", None), check_vma=False)
```
